256 devices in a mesh: az: 128 (over z, y, x), grp: 2 (over core).
Axes of the slice: x: 4, y: 4, z: 8, core: 2. Of those that a mesh axis runs over, the one named last changes fastest.
Arguments:
- features: bfloat16 [256, 512, 128], P(None, 'az', 'grp'), may hold values from -6 to 6
- cotangent: bfloat16 [256, 512, 128], P(None, 'az', 'grp'), may hold values from -6 to 6
- w_first: bfloat16 [256, 6912], P('grp'), may hold values from -0.078125 to 0.078125
- w_second: bfloat16 [256, 6912], P('grp'), may hold values from -0.078125 to 0.078125
Outputs:
- flow_out: bfloat16 [256, 512, 128], P(None, 'az', 'grp')
- grad_first: float32 [256, 6912], P('grp')
- grad_second: float32 [256, 6912], P('grp')
The draws below stay inside these ranges and needn't reach their ends.
All inputs are finite; a program needn't handle non-finite values.
Results may differ from the reference program's by a relative error of at most 0.01.
Values may be sent and summed in bfloat16 or wider, within the bound.
A program may use at most 128 MiB of HBM per device.

```python
import math
import jax
import jax.numpy as jnp
from jax import lax

CH = 256
AZ_DEV = 4
AXIAL = 8
TAPS = 6912
NAZ = 512
NRAD = 16
NRZ = 128
CELLS = 65536
N_AZ = 128


def shard_levels(own_key, extent, split, low, largest):
    factor_of = 1.0
    for position, blocks in split:
        draws = jax.random.uniform(jax.random.fold_in(jax.random.fold_in(own_key, 6), position), (blocks,), jnp.float32, low / len(split), largest / len(split))
        factor_of = factor_of * jnp.repeat(jnp.exp(draws), extent[position] // blocks).reshape((-1,) + (1,) * (len(extent) - 1 - position))
    return factor_of


def bell_draw(rng, shape, spread, most, cuts=(), held_as=jnp.bfloat16):
    level = shard_levels(rng, shape, cuts, -0.22, 0.18) if cuts else 1.0
    drawn = jax.random.normal(rng, shape, jnp.float32) * spread * level
    return jnp.minimum(jnp.maximum(drawn, -most), most).astype(held_as)


def setup_inputs(seed: int = 0) -> dict:
    keys = jax.random.split(jax.random.key(seed), 5)
    features = bell_draw(keys[0], (CH, NAZ, NRZ), 1.0, 6.0, ((1, 128), (2, 2)))
    cotangent = bell_draw(keys[1], (CH, NAZ, NRZ), 1.0, 6.0, ((1, 128), (2, 2)))
    w_first = bell_draw(keys[2], (CH, TAPS), TAPS ** -0.5, 0.078125, ((0, 2),))
    w_second = bell_draw(keys[3], (CH, TAPS), TAPS ** -0.5, 0.078125, ((0, 2),))
    return {"features": features, "cotangent": cotangent, "w_first": w_first, "w_second": w_second}


def silu_slope(values):
    sigma = jax.nn.sigmoid(values)
    return sigma * (1.0 + values * (1.0 - sigma))

def patches(padded, flipped):
    channels, span_az, span_rad, span_ax = padded.shape
    inner_az = span_az - 2
    inner_rad = span_rad - 2
    inner_ax = span_ax - 2
    stacked = []
    for along_az in range(3):
        for along_rad in range(3):
            for along_ax in range(3):
                if flipped:
                    first_az, first_rad, first_ax = (2 - along_az, 2 - along_rad, 2 - along_ax)
                else:
                    first_az, first_rad, first_ax = (along_az, along_rad, along_ax)
                stacked.append(padded[:, first_az:first_az + inner_az, first_rad:first_rad + inner_rad, first_ax:first_ax + inner_ax])
    return jnp.stack(stacked, axis=0).reshape(27 * channels, inner_az * inner_rad * inner_ax)

def pad_full(field):
    looped = jnp.concatenate([field[:, -1:], field, field[:, :1]], axis=1)
    return jnp.pad(looped, ((0, 0), (0, 0), (1, 1), (1, 1)))

def conv_full(padded, weight, flipped):

    def one_block(block):
        window = lax.dynamic_slice_in_dim(padded, block * AZ_DEV, AZ_DEV + 2, 1)
        result = jnp.dot(weight, patches(window, flipped), preferred_element_type=jnp.float32)
        return result.reshape(CH, AZ_DEV, NRZ)
    blocks = lax.map(one_block, jnp.arange(N_AZ, dtype=jnp.int32))
    return blocks.transpose(1, 0, 2, 3).reshape(CH, NAZ, NRZ)

def weight_grad(source, padded):

    def add_block(running, block):
        window = lax.dynamic_slice_in_dim(padded, block * AZ_DEV, AZ_DEV + 2, 1)
        rows_now = lax.dynamic_slice_in_dim(source, block * AZ_DEV, AZ_DEV, 1).reshape(CH, AZ_DEV * NRZ)
        update = lax.dot_general(rows_now, patches(window, False), (((1,), (1,)), ((), ())), preferred_element_type=jnp.float32)
        return (running + update, None)
    running, unused = lax.scan(add_block, jnp.zeros((CH, TAPS), jnp.float32), jnp.arange(N_AZ, dtype=jnp.int32))
    return running

def reference(features, cotangent, w_first, w_second):
    padded_in = pad_full(features.reshape(CH, NAZ, NRAD, AXIAL))
    pre_first = conv_full(padded_in, w_first, False)
    hidden = jax.nn.silu(pre_first).astype(jnp.bfloat16)
    padded_hidden = pad_full(hidden.reshape(CH, NAZ, NRAD, AXIAL))
    second = conv_full(padded_hidden, w_second, False)
    flow_out = (features.astype(jnp.float32) + second).astype(jnp.bfloat16)
    flipped_weight = w_second.reshape(CH, 27, CH).transpose(2, 1, 0).reshape(CH, 27 * CH)
    padded_cot = pad_full(cotangent.reshape(CH, NAZ, NRAD, AXIAL))
    back_grad = conv_full(padded_cot, flipped_weight, True)
    slope = (back_grad * silu_slope(pre_first)).astype(jnp.bfloat16)
    factor = 1.0 / math.sqrt(CELLS)
    grad_second = weight_grad(cotangent, padded_hidden) * factor
    grad_first = weight_grad(slope, padded_in) * factor
    return (flow_out, grad_first, grad_second)
```

```python
import functools
import math

import jax
import jax.numpy as jnp
from jax import lax
from jax.experimental import pallas as pl
from jax.experimental.pallas import tpu as pltpu
from jax.sharding import PartitionSpec as P

RAD_DEV = 8
AXIAL = 8


def with_halo(cells, sides, width, closed):
    for axis, dim in sides:
        count = lax.axis_size(axis)
        ends = count if closed else count - 1
        head = lax.slice_in_dim(cells, 0, width, axis=dim)
        tail = lax.slice_in_dim(cells, cells.shape[dim] - width, cells.shape[dim], axis=dim)
        cells = jnp.concatenate(
            [
                lax.ppermute(tail, axis, [(i, (i + 1) % count) for i in range(ends)]),
                cells,
                lax.ppermute(head, axis, [((i + 1) % count, i) for i in range(ends)]),
            ],
            axis=dim,
        )
    return cells


def silu_slope(values):
    sigma = jax.nn.sigmoid(values)
    return sigma * (1.0 + values * (1.0 - sigma))


def patches(padded, flipped):
    channels, span_az, span_rad, span_ax = padded.shape
    inner_az = span_az - 2
    inner_rad = span_rad - 2
    inner_ax = span_ax - 2
    stacked = []
    for along_az in range(3):
        for along_rad in range(3):
            for along_ax in range(3):
                if flipped:
                    first_az, first_rad, first_ax = (2 - along_az, 2 - along_rad, 2 - along_ax)
                else:
                    first_az, first_rad, first_ax = (along_az, along_rad, along_ax)
                stacked.append(
                    padded[
                        :,
                        first_az : first_az + inner_az,
                        first_rad : first_rad + inner_rad,
                        first_ax : first_ax + inner_ax,
                    ]
                )
    return jnp.stack(stacked, axis=0).reshape(27 * channels, inner_az * inner_rad * inner_ax)


def az_rim(field):
    return with_halo(field, (("az", 1),), 1, True)


def radial_rim(field):
    return with_halo(field, (("grp", 2),), 1, False)


def axial_pad(field):
    return jnp.pad(field, ((0, 0), (0, 0), (0, 0), (1, 1)))


def flip_weight(weight):
    rows_here = weight.shape[0]
    channels = weight.shape[1] // 27
    return (
        weight.reshape(rows_here, 27, channels).transpose(2, 1, 0).reshape(channels, 27 * rows_here)
    )


def contract_cells(left, right):
    return lax.dot_general(
        left, right, (((1,), (1,)), ((), ())), preferred_element_type=jnp.float32
    )


def rows_forward(weight, columns):
    return jnp.dot(
        lax.all_gather(weight, "grp", axis=0, tiled=True),
        columns,
        preferred_element_type=jnp.float32,
    )


def group_grad(source, columns):
    return lax.psum_scatter(
        contract_cells(source, columns).astype(jnp.bfloat16), "grp", scatter_dimension=0, tiled=True
    )


NX, NY, NZ = 4, 4, 8
EXTENT = {"x": NX, "y": NY, "z": NZ}
TAP_LANES = 128
PARTS = (
    ("z", "y", "x", 0, 4, True),
    ("z", "y", "x", 4, 3, False),
    ("x", "z", "y", 7, 5, True),
    ("x", "z", "y", 12, 5, False),
    ("y", "z", "x", 17, 5, True),
    ("y", "z", "x", 22, 5, False),
)


def chain_lengths(axis, longer_below):
    count = EXTENT[axis]
    longer, shorter = count // 2, count - 1 - count // 2
    return (longer, shorter) if longer_below else (shorter, longer)


def chunk_shape(axes_done, axis, taps):
    rows = 16 if "z" in axes_done + (axis,) else 128
    lead = () if ("x" in axes_done + (axis,) or "y" in axes_done + (axis,)) else (4,)
    return lead + (rows, taps * TAP_LANES)


class Links:
    def __init__(self, send_sems, recv_sems):
        self.send_sems, self.recv_sems, self.used, self.started = send_sems, recv_sems, 0, []
        flat = lax.axis_index("az")
        self.at = {"x": flat % NX, "y": (flat // NX) % NY, "z": flat // (NX * NY)}

    def index(self, axis, shift):
        return (self.at[axis] + (shift + EXTENT[axis])) % EXTENT[axis]

    def peer(self, axis, shift):
        to = dict(self.at)
        to[axis] = self.index(axis, shift)
        return {"az": (to["z"] * NY + to["y"]) * NX + to["x"]}

    def copy(self, source, target, axis, shift):
        number = self.used
        self.used += 1
        handle = pltpu.make_async_remote_copy(
            src_ref=source,
            dst_ref=target,
            send_sem=self.send_sems.at[number],
            recv_sem=self.recv_sems.at[number],
            device_id=self.peer(axis, shift),
            device_id_type=pl.DeviceIdType.MESH,
        )
        handle.start()
        self.started.append(handle)
        return handle


def piece(ref, axes, at, lanes):
    rows = pl.ds(0, 128)
    if "z" in axes:
        rows = pl.ds(pl.multiple_of(at["z"] * 16, 16), 16)
    lead = [a for a in axes if a != "z"]
    first = at[lead[0]] if lead else slice(None)
    return ref.at[first, rows, lanes]


def scatter_axis(links, axis, longer_below, own, buffers):
    below, above = chain_lengths(axis, longer_below)
    ways = [(1, below, buffers[0], buffers[1]), (-1, above, buffers[2], buffers[3])]
    last = {}
    for step in range(1, max(below, above) + 1):
        for sense, length, stage, landing in ways:
            if step > length:
                continue
            total = own(links.index(axis, sense * (length - step + 1)))
            if step > 1:
                last[sense].wait_recv()
                total = total + landing[step - 2].astype(jnp.float32)
            stage[step - 1] = total.astype(jnp.bfloat16)
            last[sense] = links.copy(stage.at[step - 1], landing.at[step - 1], axis, sense)
        yield
    total = own(links.at[axis])
    for sense, length, stage, landing in ways:
        last[sense].wait_recv()
        total = total + landing[length - 1].astype(jnp.float32)
    return total


def gather_axis(links, axis, longer_below, view):
    below, above = chain_lengths(axis, longer_below)
    last = {}
    for step in range(1, max(below, above) + 1):
        for sense, length in ((1, below), (-1, above)):
            if step > length:
                continue
            if step > 1:
                last[sense].wait_recv()
            chunk = view(links.index(axis, -sense * (step - 1)))
            last[sense] = links.copy(chunk, chunk, axis, sense)
        yield
    for sense in (1, -1):
        last[sense].wait_recv()


def reduce_part(links, part, source, result, buffers):
    first, second, third, tap, taps, longer_below = part
    lanes = pl.ds(tap * TAP_LANES, taps * TAP_LANES)
    one, two, three = buffers[:5], buffers[5:10], buffers[10:]

    def own_first(index):
        return piece(source, (first,), {first: index}, lanes)[...].astype(jnp.float32)

    total = yield from scatter_axis(links, first, longer_below, own_first, one[:4])
    one[4][...] = total

    def own_second(index):
        if second == "z":
            return one[4][pl.ds(pl.multiple_of(index * 16, 16), 16), :]
        return one[4][index]

    total = yield from scatter_axis(links, second, not longer_below, own_second, two[:4])
    mine, landing = three
    landing[links.at[third]] = total.astype(jnp.bfloat16)
    handles = [
        links.copy(landing.at[links.at[third]], landing.at[links.at[third]], third, shift)
        for shift in (1, -1, 2)
    ]
    yield
    for handle in handles:
        handle.wait_recv()
    total = landing[0].astype(jnp.float32)
    for index in range(1, EXTENT[third]):
        total = total + landing[index].astype(jnp.float32)
    piece(result, (first, second), links.at, lanes)[...] = total.astype(jnp.bfloat16)
    at = links.at
    yield from gather_axis(
        links,
        second,
        longer_below,
        lambda index: piece(result, (first, second), {**at, second: index}, lanes),
    )
    yield from gather_axis(
        links,
        first,
        not longer_below,
        lambda index: piece(result, (first,), {**at, first: index}, lanes),
    )


def part_scratch(part):
    first, second, third, tap, taps, longer_below = part
    shapes = []
    one = chunk_shape((), first, taps)
    two = chunk_shape((first,), second, taps)
    for axis, shape, flag in ((first, one, longer_below), (second, two, not longer_below)):
        below, above = chain_lengths(axis, flag)
        for length in (below, below, above, above):
            shapes.append(pltpu.VMEM((length,) + shape, jnp.bfloat16))
        shapes.append(pltpu.VMEM(shape, jnp.float32))
    shapes.append(pltpu.VMEM((8, 128), jnp.float32))
    shapes.append(pltpu.VMEM((EXTENT[third],) + two, jnp.bfloat16))
    return shapes


def greet(links):
    barrier = pltpu.get_barrier_semaphore()
    peers = [("z", 1), ("z", -1)] + [(axis, shift) for axis in "xy" for shift in (1, -1, 2)]
    for axis, shift in peers:
        pl.semaphore_signal(
            barrier,
            inc=1,
            device_id=links.peer(axis, shift),
            device_id_type=pl.DeviceIdType.MESH,
        )
    pl.semaphore_wait(barrier, len(peers))


COPIES = 256


def reduce_kernel(source, result, send_sems, recv_sems, *buffers):
    links = Links(send_sems, recv_sems)
    greet(links)
    running, used = [], 0
    for part in PARTS:
        count = len(part_scratch(part))
        running.append(reduce_part(links, part, source, result, buffers[used : used + count]))
        used += count
    while running:
        left = []
        for one in running:
            try:
                next(one)
                left.append(one)
            except StopIteration:
                pass
        running = left
    for handle in links.started:
        handle.wait_send()


def reduce_over_az(terms):
    scratch = [pltpu.SemaphoreType.DMA((COPIES,)), pltpu.SemaphoreType.DMA((COPIES,))]
    for part in PARTS:
        scratch += part_scratch(part)
    return pl.pallas_call(
        reduce_kernel,
        out_shape=jax.ShapeDtypeStruct(terms.shape, jnp.bfloat16),
        in_specs=[pl.BlockSpec(memory_space=pltpu.VMEM)],
        out_specs=pl.BlockSpec(memory_space=pltpu.VMEM),
        scratch_shapes=scratch,
        compiler_params=pltpu.CompilerParams(
            collective_id=0, has_side_effects=True, vmem_limit_bytes=40 * 2**20
        ),
        name="reduce_over_az",
    )(terms)


def local(features, cotangent, w_first, w_second):
    channels, az_cells, flat_cells = features.shape
    groups = lax.axis_size("grp")
    cell_count = az_cells * RAD_DEV * AXIAL
    factor = 1.0 / math.sqrt(az_cells * lax.axis_size("az") * RAD_DEV * groups * AXIAL)
    field_in = features.reshape(channels, az_cells, RAD_DEV, AXIAL)
    field_cot = cotangent.reshape(channels, az_cells, RAD_DEV, AXIAL)
    input_columns = patches(axial_pad(radial_rim(az_rim(field_in))), False)
    pre_first = rows_forward(w_first, input_columns).reshape(channels, az_cells, flat_cells)
    hidden = jax.nn.silu(pre_first).astype(jnp.bfloat16)
    hidden_columns = patches(
        axial_pad(radial_rim(az_rim(hidden.reshape(channels, az_cells, RAD_DEV, AXIAL)))), False
    )
    second = rows_forward(w_second, hidden_columns).reshape(channels, az_cells, flat_cells)
    flow_out = (features.astype(jnp.float32) + second).astype(jnp.bfloat16)
    cot_columns = patches(axial_pad(radial_rim(az_rim(field_cot))), True).reshape(
        27, channels, cell_count
    )
    weight_piece = lax.all_gather(w_second, "grp", axis=0, tiled=True)
    piece_rows = weight_piece.shape[0]
    turned = flip_weight(weight_piece)
    picked = cot_columns.reshape(27 * piece_rows, cell_count)
    back_grad = jnp.dot(turned, picked, preferred_element_type=jnp.float32)
    slope = (back_grad * silu_slope(pre_first.reshape(channels, cell_count))).astype(jnp.bfloat16)
    grad_second = group_grad(cotangent.reshape(channels, cell_count), hidden_columns)
    grad_first = group_grad(slope, input_columns)
    rows = grad_first.shape[0]
    terms = jnp.stack((grad_first, grad_second)).reshape(2, rows, 27, 2, 128)
    summed = reduce_over_az(terms.transpose(0, 3, 1, 2, 4).reshape(4, rows, 27 * 128))
    summed = summed.reshape(2, 2, rows, 27, 128).transpose(0, 2, 3, 1, 4).reshape(2, rows, 6912)
    summed = summed.astype(jnp.float32) * factor
    return (flow_out, summed[0], summed[1])


def solution(mesh):
    in_specs = (P(None, "az", "grp"), P(None, "az", "grp"), P("grp", None), P("grp", None))
    out_specs = (P(None, "az", "grp"), P("grp", None), P("grp", None))
    return jax.shard_map(local, mesh=mesh, in_specs=in_specs, out_specs=out_specs, check_vma=False)
```

```python
import functools
import math

import jax
import jax.numpy as jnp
from jax import lax
from jax.experimental import pallas as pl
from jax.experimental.pallas import tpu as pltpu
from jax.sharding import PartitionSpec as P

CH = 256
HALF = 128
TAPS = 27
RAD = 16
AXIAL = 8
AZ_DEV = 4
ROWS = RAD * AXIAL
OWN_ROWS = ROWS // 2
CELLS_CHIP = AZ_DEV * ROWS

NX, NY, NZ = 4, 4, 8
EXTENT = {"x": NX, "y": NY, "z": NZ}
TAP_LANES = 128
PARTS = (
    ("z", "y", "x", 0, 5, True),
    ("z", "y", "x", 5, 4, False),
    ("x", "z", "y", 9, 5, True),
    ("x", "z", "y", 14, 4, False),
    ("y", "z", "x", 18, 5, True),
    ("y", "z", "x", 23, 4, False),
)


def chain_lengths(axis, longer_below):
    count = EXTENT[axis]
    longer, shorter = count // 2, count - 1 - count // 2
    return (longer, shorter) if longer_below else (shorter, longer)


def chunk_shape(axes_done, axis, taps):
    rows = 16 if "z" in axes_done + (axis,) else 128
    lead = () if ("x" in axes_done + (axis,) or "y" in axes_done + (axis,)) else (4,)
    return lead + (rows, taps * TAP_LANES)


class Links:
    def __init__(self, send_sems, recv_sems):
        self.send_sems, self.recv_sems, self.used, self.started = send_sems, recv_sems, 0, []
        flat = lax.axis_index("az")
        self.flat, self.core = flat, lax.axis_index("grp")
        self.at = {"x": flat % NX, "y": (flat // NX) % NY, "z": flat // (NX * NY)}

    def index(self, axis, shift):
        return (self.at[axis] + (shift + EXTENT[axis])) % EXTENT[axis]

    def peer(self, axis, shift):
        to = dict(self.at)
        to[axis] = self.index(axis, shift)
        return {"az": (to["z"] * NY + to["y"]) * NX + to["x"], "grp": self.core}

    def beside(self, shift, core):
        count = NX * NY * NZ
        return {"az": (self.flat + (shift + count)) % count, "grp": core}

    def copy(self, source, target, axis, shift):
        return self.send(source, target, self.peer(axis, shift))

    def send(self, source, target, device):
        number = self.used
        self.used += 1
        handle = pltpu.make_async_remote_copy(
            src_ref=source,
            dst_ref=target,
            send_sem=self.send_sems.at[number],
            recv_sem=self.recv_sems.at[number],
            device_id=device,
            device_id_type=pl.DeviceIdType.MESH,
        )
        handle.start()
        self.started.append(handle)
        return handle


def piece(ref, axes, at, lanes):
    rows = pl.ds(0, 128)
    if "z" in axes:
        rows = pl.ds(pl.multiple_of(at["z"] * 16, 16), 16)
    lead = [a for a in axes if a != "z"]
    first = at[lead[0]] if lead else slice(None)
    return ref.at[first, rows, lanes]


def scatter_axis(links, axis, longer_below, own, buffers):
    below, above = chain_lengths(axis, longer_below)
    ways = [(1, below, buffers[0], buffers[1]), (-1, above, buffers[2], buffers[3])]
    last = {}
    for step in range(1, max(below, above) + 1):
        for sense, length, stage, landing in ways:
            if step > length:
                continue
            total = own(links.index(axis, sense * (length - step + 1)))
            if step > 1:
                last[sense].wait_recv()
                total = total + landing[step - 2].astype(jnp.float32)
            stage[step - 1] = total.astype(jnp.bfloat16)
            last[sense] = links.copy(stage.at[step - 1], landing.at[step - 1], axis, sense)
        yield
    total = own(links.at[axis])
    for sense, length, stage, landing in ways:
        last[sense].wait_recv()
        total = total + landing[length - 1].astype(jnp.float32)
    return total


def gather_axis(links, axis, longer_below, view):
    below, above = chain_lengths(axis, longer_below)
    last = {}
    for step in range(1, max(below, above) + 1):
        for sense, length in ((1, below), (-1, above)):
            if step > length:
                continue
            if step > 1:
                last[sense].wait_recv()
            chunk = view(links.index(axis, -sense * (step - 1)))
            last[sense] = links.copy(chunk, chunk, axis, sense)
        yield
    for sense in (1, -1):
        last[sense].wait_recv()


def reduce_part(links, part, source, result, buffers):
    first, second, third, tap, taps, longer_below = part
    lanes = pl.ds(tap * TAP_LANES, taps * TAP_LANES)
    one, two, three = buffers[:5], buffers[5:10], buffers[10:]

    def own_first(index):
        return piece(source, (first,), {first: index}, lanes)[...].astype(jnp.float32)

    total = yield from scatter_axis(links, first, longer_below, own_first, one[:4])
    one[4][...] = total

    def own_second(index):
        if second == "z":
            return one[4][pl.ds(pl.multiple_of(index * 16, 16), 16), :]
        return one[4][index]

    total = yield from scatter_axis(links, second, not longer_below, own_second, two[:4])
    mine, landing = three
    landing[links.at[third]] = total.astype(jnp.bfloat16)
    handles = [
        links.copy(landing.at[links.at[third]], landing.at[links.at[third]], third, shift)
        for shift in (1, -1, 2)
    ]
    yield
    for handle in handles:
        handle.wait_recv()
    total = landing[0].astype(jnp.float32)
    for index in range(1, EXTENT[third]):
        total = total + landing[index].astype(jnp.float32)
    piece(result, (first, second), links.at, lanes)[...] = total.astype(jnp.bfloat16)
    at = links.at
    yield from gather_axis(
        links,
        second,
        longer_below,
        lambda index: piece(result, (first, second), {**at, second: index}, lanes),
    )
    yield from gather_axis(
        links,
        first,
        not longer_below,
        lambda index: piece(result, (first,), {**at, first: index}, lanes),
    )


def part_scratch(part):
    first, second, third, tap, taps, longer_below = part
    shapes = []
    one = chunk_shape((), first, taps)
    two = chunk_shape((first,), second, taps)
    for axis, shape, flag in ((first, one, longer_below), (second, two, not longer_below)):
        below, above = chain_lengths(axis, flag)
        for length in (below, below, above, above):
            shapes.append(pltpu.VMEM((length,) + shape, jnp.bfloat16))
        shapes.append(pltpu.VMEM(shape, jnp.float32))
    shapes.append(pltpu.VMEM((8, 128), jnp.float32))
    shapes.append(pltpu.VMEM((EXTENT[third],) + two, jnp.bfloat16))
    return shapes


def greet(links):
    barrier = pltpu.get_barrier_semaphore()
    peers = [links.peer("z", 1), links.peer("z", -1), links.beside(0, 1 - links.core)]
    peers += [links.peer(axis, shift) for axis in "xy" for shift in (1, -1, 2)]
    peers += [
        links.beside(shift, core) for shift in (1, -1) for core in (links.core, 1 - links.core)
    ]
    for device in peers:
        pl.semaphore_signal(
            barrier, inc=1, device_id=device, device_id_type=pl.DeviceIdType.MESH
        )
    pl.semaphore_wait(barrier, len(peers))


def shifted_copies(level, padded):
    channels = level.shape[3]
    along = lax.broadcasted_iota(jnp.int32, (RAD, AXIAL, channels), 1)
    rim = jnp.zeros((AXIAL, channels), jnp.bfloat16).astype(jnp.float32)

    def one_slab(slab, carry):
        here = level[1, slab].astype(jnp.float32).reshape(RAD, AXIAL, channels)
        below = jnp.where(along == 0, 0.0, pltpu.roll(here, 1, 1))
        above = jnp.where(along == AXIAL - 1, 0.0, pltpu.roll(here, AXIAL - 1, 1))
        for offset, values in ((0, below), (1, here), (2, above)):
            rows = values.reshape(ROWS, channels)
            if offset != 1:
                level[offset, slab] = rows.astype(jnp.bfloat16)
            padded[offset, slab] = jnp.concatenate((rim, rows, rim), axis=0).astype(jnp.bfloat16)
        return carry

    lax.fori_loop(0, AZ_DEV + 2, one_slab, 0)


def window(level, padded, along_az, along_rad, along_ax):
    channels = level.shape[3]
    slabs = pl.ds(along_az, AZ_DEV)
    if along_rad == 1:
        picked = level[along_ax, slabs]
    else:
        picked = padded[along_ax, slabs, pl.ds(AXIAL * along_rad, ROWS), :]
    return picked.reshape(CELLS_CHIP, channels)


def tap_lanes(along_az, along_rad, along_ax, width):
    tap = (along_az * 3 + along_rad) * 3 + along_ax
    return pl.ds(pl.multiple_of(tap * width, width), width)


def convolve(level, padded, weight, total):
    total[...] = jnp.zeros_like(total)

    def one_step(step, carry):
        along_az, along_ax = step // 3, step % 3
        added = total[...]
        for along_rad in range(3):
            added = added + lax.dot_general(
                window(level, padded, along_az, along_rad, along_ax),
                weight[:, tap_lanes(along_az, along_rad, along_ax, CH)],
                (((1,), (1,)), ((), ())),
                preferred_element_type=jnp.float32,
            )
        total[...] = added
        return carry

    lax.fori_loop(0, 9, one_step, 0)


def convolve_back(level, padded, weight, total):
    total[...] = jnp.zeros_like(total)

    def one_step(step, carry):
        along_az, along_ax = step // 3, step % 3
        columns = jnp.concatenate(
            [window(level, padded, 2 - along_az, 2 - rad, 2 - along_ax) for rad in range(3)], axis=1
        )
        rows = jnp.concatenate(
            [weight[:, tap_lanes(along_az, rad, along_ax, CH)] for rad in range(3)], axis=0
        )
        update = jnp.dot(columns, rows, preferred_element_type=jnp.float32)
        for side in range(2):
            total[side] = total[side] + update[:, side * HALF : (side + 1) * HALF]
        return carry

    lax.fori_loop(0, 9, one_step, 0)


def weight_terms(turned, level, padded, terms, which, along_az):
    def one_step(along_ax, carry):
        for along_rad in range(3):
            update = jnp.dot(
                turned[...],
                window(level, padded, along_az, along_rad, along_ax),
                preferred_element_type=jnp.float32,
            )
            lanes = tap_lanes(along_az, along_rad, along_ax, HALF)
            for side in range(2):
                terms[2 * which + side, :, lanes] = update[:, side * HALF : (side + 1) * HALF]
        return carry

    lax.fori_loop(0, 3, one_step, 0)


def flow_part(links, features, level, padded, weight, total, mine, flow):
    core = links.core
    lanes = pl.ds(pl.multiple_of(core * HALF, HALF), HALF)
    convolve(level, padded, weight, total)
    yield
    own = features[1, pl.ds(1, AZ_DEV), :, lanes].astype(jnp.float32)
    mine[...] = (own + total[...].reshape(AZ_DEV, ROWS, HALF)).astype(jnp.bfloat16)
    here = pl.ds(pl.multiple_of(core * OWN_ROWS, OWN_ROWS), OWN_ROWS)
    there = pl.ds(pl.multiple_of((1 - core) * OWN_ROWS, OWN_ROWS), OWN_ROWS)
    flow[:, :, lanes] = mine[:, here, :]
    handle = links.send(mine.at[:, there, :], flow.at[:, :, lanes], links.beside(0, 1 - core))
    yield
    handle.wait_recv()


def exchange_rims(links, source, target, rows):
    core = links.core
    handles = []
    for to in (1 - core, core):
        for shift, slab, landing in ((1, AZ_DEV - 1, 0), (-1, 0, AZ_DEV + 1)):
            given, taken = source(slab, to), target(landing, to)
            handles.append(links.send(given, taken, links.beside(shift, to)))
        if to is not core:
            handles.append(
                links.send(
                    source(slice(None), to), target(pl.ds(1, AZ_DEV), to), links.beside(0, to)
                )
            )
    return handles


def whole_kernel(
    features,
    cotangent,
    w_first,
    w_second,
    flow,
    result,
    send_sems,
    recv_sems,
    local_sems,
    first_rows,
    second_rows,
    in_level,
    in_padded,
    cot_level,
    cot_padded,
    hid_level,
    hid_padded,
    pre,
    second,
    back,
    back_other,
    turned,
    mine,
    terms,
    *buffers,
):
    links = Links(send_sems, recv_sems)
    core = links.core
    here = pl.ds(pl.multiple_of(core * OWN_ROWS, OWN_ROWS), OWN_ROWS)
    cells = pl.ds(1, AZ_DEV)

    def lanes(which):
        return pl.ds(pl.multiple_of(which * HALF, HALF), HALF)

    loads = [
        pltpu.make_async_copy(*pair, local_sems.at[number])
        for number, pair in enumerate(
            (
                (features, in_level.at[1, cells, here, :]),
                (cotangent.at[:, :, lanes(core)], cot_level.at[1, cells, here, :]),
                (w_first, first_rows),
                (w_second, second_rows),
            )
        )
    ]
    for load in loads:
        load.start()
    greet(links)
    field_in = exchange_rims(
        links,
        lambda slab, to: features.at[slab],
        lambda slab, to: in_level.at[1, slab, here, :],
        here,
    )
    field_cot = exchange_rims(
        links,
        lambda slab, to: cotangent.at[slab, :, lanes(to)],
        lambda slab, to: cot_level.at[1, slab, here, :],
        here,
    )
    loads[0].wait()
    loads[2].wait()
    for handle in field_in:
        handle.wait_recv()
    shifted_copies(in_level, in_padded)
    convolve(in_level, in_padded, first_rows, pre)
    values = pre[...]
    hidden = values * jax.nn.sigmoid(values)
    hid_level[1, cells, :, lanes(core)] = hidden.astype(jnp.bfloat16).reshape(AZ_DEV, ROWS, HALF)
    field_hid = exchange_rims(
        links,
        lambda slab, to: hid_level.at[
            1, pl.ds(1, AZ_DEV) if isinstance(slab, slice) else slab + 1, :, lanes(core)
        ],
        lambda slab, to: hid_level.at[1, slab, :, lanes(core)],
        here,
    )
    loads[1].wait()
    loads[3].wait()
    for handle in field_cot:
        handle.wait_recv()
    shifted_copies(cot_level, cot_padded)
    convolve_back(cot_level, cot_padded, second_rows, back)
    swap = links.send(back.at[1 - core], back_other, links.beside(0, 1 - core))
    own_cot = cot_level[1, cells].reshape(CELLS_CHIP, HALF).astype(jnp.float32)
    turned[1] = own_cot.T.astype(jnp.bfloat16)
    swap.wait_recv()
    values = pre[...]
    sigma = jax.nn.sigmoid(values)
    slope = (back[core] + back_other[...]) * (sigma * (1.0 + values * (1.0 - sigma)))
    turned[0] = slope.T.astype(jnp.bfloat16)
    for along_az in range(3):
        weight_terms(turned.at[0], in_level, in_padded, terms, 0, along_az)
    for handle in field_hid:
        handle.wait_recv()
    shifted_copies(hid_level, hid_padded)
    running, used = [], 0

    def advance():
        for one in list(running):
            try:
                next(one)
            except StopIteration:
                running.remove(one)

    for number, part in enumerate(PARTS):
        if part[3] % 9 == 0:
            weight_terms(turned.at[1], hid_level, hid_padded, terms, 1, part[3] // 9)
            advance()
        count = len(part_scratch(part))
        running.append(reduce_part(links, part, terms, result, buffers[used : used + count]))
        used += count
        next(running[-1])
    running.append(
        flow_part(links, in_level, hid_level, hid_padded, second_rows, second, mine, flow)
    )
    while running:
        advance()
    for handle in links.started:
        handle.wait_send()


COPIES = 192


def whole_layer(features, cotangent, w_first, w_second):
    field = (3, AZ_DEV + 2, ROWS)
    padded = (3, AZ_DEV + 2, ROWS + 2 * AXIAL)
    scratch = [
        pltpu.SemaphoreType.DMA((COPIES,)),
        pltpu.SemaphoreType.DMA((COPIES,)),
        pltpu.SemaphoreType.DMA((4,)),
        pltpu.VMEM((HALF, TAPS * CH), jnp.bfloat16),
        pltpu.VMEM((HALF, TAPS * CH), jnp.bfloat16),
        pltpu.VMEM(field + (CH,), jnp.bfloat16),
        pltpu.VMEM(padded + (CH,), jnp.bfloat16),
        pltpu.VMEM(field + (HALF,), jnp.bfloat16),
        pltpu.VMEM(padded + (HALF,), jnp.bfloat16),
        pltpu.VMEM(field + (CH,), jnp.bfloat16),
        pltpu.VMEM(padded + (CH,), jnp.bfloat16),
        pltpu.VMEM((CELLS_CHIP, HALF), jnp.float32),
        pltpu.VMEM((CELLS_CHIP, HALF), jnp.float32),
        pltpu.VMEM((2, CELLS_CHIP, HALF), jnp.float32),
        pltpu.VMEM((CELLS_CHIP, HALF), jnp.float32),
        pltpu.VMEM((2, HALF, CELLS_CHIP), jnp.bfloat16),
        pltpu.VMEM((AZ_DEV, ROWS, HALF), jnp.bfloat16),
        pltpu.VMEM((4, HALF, TAPS * HALF), jnp.float32),
    ]
    for part in PARTS:
        scratch += part_scratch(part)
    return pl.pallas_call(
        whole_kernel,
        out_shape=(
            jax.ShapeDtypeStruct((AZ_DEV, OWN_ROWS, CH), jnp.bfloat16),
            jax.ShapeDtypeStruct((4, HALF, TAPS * HALF), jnp.bfloat16),
        ),
        in_specs=[pl.BlockSpec(memory_space=pl.ANY)] * 4,
        out_specs=(pl.BlockSpec(memory_space=pltpu.VMEM), pl.BlockSpec(memory_space=pltpu.VMEM)),
        scratch_shapes=scratch,
        compiler_params=pltpu.CompilerParams(
            collective_id=0, has_side_effects=True, vmem_limit_bytes=56 * 2**20
        ),
        name="both_layers",
    )(features, cotangent, w_first, w_second)


def widen_kernel(factor, summed, grad_first, grad_second):
    def put(target):
        for tap in range(9):
            for side in range(2):
                target[:, (2 * tap + side) * HALF : (2 * tap + side + 1) * HALF] = (
                    summed[side, :, tap * HALF : (tap + 1) * HALF].astype(jnp.float32) * factor
                )

    @pl.when(pl.program_id(0) == 0)
    def _():
        put(grad_first)

    @pl.when(pl.program_id(0) == 1)
    def _():
        put(grad_second)


def widen(summed, factor):
    third = TAPS * CH // 3
    shape = jax.ShapeDtypeStruct((HALF, TAPS * CH), jnp.float32)
    return pl.pallas_call(
        functools.partial(widen_kernel, factor),
        grid=(2, 3),
        out_shape=(shape, shape),
        in_specs=[pl.BlockSpec((2, HALF, third // 2), lambda g, p: (g, 0, p))],
        out_specs=(
            pl.BlockSpec((HALF, third), lambda g, p: (0, jnp.where(g == 0, p, 2))),
            pl.BlockSpec((HALF, third), lambda g, p: (0, jnp.where(g == 0, 0, p))),
        ),
        compiler_params=pltpu.CompilerParams(vmem_limit_bytes=24 * 2**20),
        name="widen",
    )(summed)


def local(features, cotangent, w_first, w_second):
    factor = 1.0 / math.sqrt(NX * NY * NZ * CELLS_CHIP)
    flow, summed = whole_layer(
        features.transpose(1, 2, 0), cotangent.transpose(1, 2, 0), w_first, w_second
    )
    grad_first, grad_second = widen(summed, factor)
    return (flow.transpose(2, 0, 1), grad_first, grad_second)


def solution(mesh):
    in_specs = (P(None, "az", "grp"), P(None, "az", "grp"), P("grp", None), P("grp", None))
    out_specs = (P(None, "az", "grp"), P("grp", None), P("grp", None))
    return jax.shard_map(local, mesh=mesh, in_specs=in_specs, out_specs=out_specs, check_vma=False)
```

```python
import functools
import math

import jax
import jax.numpy as jnp
from jax import lax
from jax.experimental import pallas as pl
from jax.experimental.pallas import tpu as pltpu
from jax.sharding import PartitionSpec as P

CH = 256
HALF = 128
TAPS = 27
RAD = 16
AXIAL = 8
AZ_DEV = 4
ROWS = RAD * AXIAL
OWN_ROWS = ROWS // 2
CELLS_CHIP = AZ_DEV * ROWS

NX, NY, NZ = 4, 4, 8
EXTENT = {"x": NX, "y": NY, "z": NZ}
TAP_LANES = 128
PARTS = (
    ("x", "y", 0, 5, 1),
    ("y", "x", 5, 4, 1),
    ("y", "x", 9, 5, -1),
    ("x", "y", 14, 4, -1),
    ("x", "y", 18, 5, 1),
    ("y", "x", 23, 4, 1),
)


BYTES_PER_US = 65000.0
SEND_US, HOP_US, STEP_US, CONVOLVE_US = 1.5, 0.3, 0.15, 0.45


class Links:
    def __init__(self, send_sems, recv_sems):
        self.send_sems, self.recv_sems, self.used, self.started = send_sems, recv_sems, 0, []
        self.now, self.busy = 0.0, {}
        flat = lax.axis_index("az")
        self.flat, self.core = flat, lax.axis_index("grp")
        self.at = {"x": flat % NX, "y": (flat // NX) % NY, "z": flat // (NX * NY)}

    def index(self, axis, shift):
        return (self.at[axis] + (shift + EXTENT[axis])) % EXTENT[axis]

    def peer(self, axis, shift):
        to = dict(self.at)
        to[axis] = self.index(axis, shift)
        return {"az": (to["z"] * NY + to["y"]) * NX + to["x"], "grp": self.core}

    def beside(self, shift, core):
        count = NX * NY * NZ
        return {"az": (self.flat + (shift + count)) % count, "grp": core}

    def copy(self, source, target, axis, shift):
        lane, hops = (axis, shift > 0), abs(shift)
        begin = max(self.now, self.busy.get(lane, 0.0))
        self.busy[lane] = begin + hops * 2 * math.prod(source.shape) / BYTES_PER_US
        handle = self.send(source, target, self.peer(axis, shift))
        return handle, self.busy[lane] + SEND_US + HOP_US * hops

    def send(self, source, target, device):
        number = self.used
        self.used += 1
        handle = pltpu.make_async_remote_copy(
            src_ref=source,
            dst_ref=target,
            send_sem=self.send_sems.at[number],
            recv_sem=self.recv_sems.at[number],
            device_id=device,
            device_id_type=pl.DeviceIdType.MESH,
        )
        handle.start()
        self.started.append(handle)
        return handle


def piece(ref, axes, at, lanes):
    rows = pl.ds(0, 128)
    if "z" in axes:
        rows = pl.ds(pl.multiple_of(at["z"] * 16, 16), 16)
    lead = [a for a in axes if a != "z"]
    first = at[lead[0]] if lead else slice(None)
    return ref.at[first, rows, lanes]


ROUTES = {4: ((2, 1), (-1, -1)), 8: ((4, 1), (2, 1), (-3, -1), (-1, -1))}


def relays(axis):
    return [(owner - stop, stop) for owner, stop in ROUTES[EXTENT[axis]] if owner != stop]


def arrivals(axis):
    routes = ROUTES[EXTENT[axis]]
    return [onward for onward, _ in relays(axis)] + [o for o, stop in routes if o == stop]


def scatter_axis(links, axis, sense, own, stage, landing):
    first = []
    for slot, (owner, stop) in enumerate(ROUTES[EXTENT[axis]]):
        stage[slot] = own(links.index(axis, sense * owner)).astype(jnp.bfloat16)
        first.append(links.copy(stage.at[slot], landing.at[slot], axis, sense * stop))
    last = []
    slot = len(first)
    for number, (owner, stop) in enumerate(ROUTES[EXTENT[axis]]):
        handle, due = first[number]
        if owner == stop:
            last.append((number, handle, due))
            continue
        onward = owner - stop
        total = own(links.index(axis, sense * onward))
        yield due
        handle.wait_recv()
        stage[slot] = (total + landing[number].astype(jnp.float32)).astype(jnp.bfloat16)
        last.append((slot,) + links.copy(stage.at[slot], landing.at[slot], axis, sense * onward))
        slot += 1
    total = own(links.at[axis])
    yield max(due for _, _, due in last)
    for slot, handle, _ in last:
        handle.wait_recv()
        total = total + landing[slot].astype(jnp.float32)
    return total


def gather_axis(links, axis, sense, view):
    chunk = view(links.at[axis])
    first = [
        (onward,) + links.copy(chunk, chunk, axis, sense * onward) for onward in arrivals(axis)
    ]
    last = []
    for number, (onward, stop) in enumerate(relays(axis)):
        _, handle, due = first[number]
        yield due
        handle.wait_recv()
        chunk = view(links.index(axis, -sense * onward))
        last.append(links.copy(chunk, chunk, axis, sense * stop))
    last += [(handle, due) for _, handle, due in first[len(last) :]]
    yield max(due for _, due in last)
    for handle, _ in last:
        handle.wait_recv()


def reduce_part(links, part, source, result, buffers):
    first, third, tap, taps, sense = part
    lanes = pl.ds(tap * TAP_LANES, taps * TAP_LANES)
    stage_one, landing_one, sum_one, stage_two, landing_two, landing_three = buffers

    def own_first(index):
        return source[index, :, lanes]

    sum_one[...] = yield from scatter_axis(
        links, first, sense, own_first, stage_one, landing_one
    )

    def own_second(index):
        return sum_one[pl.ds(pl.multiple_of(index * 16, 16), 16), :]

    total = yield from scatter_axis(links, "z", -sense, own_second, stage_two, landing_two)
    mine = landing_three.at[links.at[third]]
    mine[...] = total.astype(jnp.bfloat16)
    sent = [links.copy(mine, mine, third, shift) for shift in (1, -1, 2)]
    yield max(due for _, due in sent)
    for handle, _ in sent:
        handle.wait_recv()
    total = landing_three[0].astype(jnp.float32)
    for index in range(1, EXTENT[third]):
        total = total + landing_three[index].astype(jnp.float32)
    at = links.at
    piece(result, (first, "z"), at, lanes)[...] = total.astype(jnp.bfloat16)
    yield from gather_axis(
        links, "z", sense, lambda index: piece(result, (first, "z"), {**at, "z": index}, lanes)
    )
    yield from gather_axis(
        links, first, -sense, lambda index: piece(result, (first,), {first: index}, lanes)
    )


def part_scratch(part):
    first, third, tap, taps, sense = part
    one, two = (128, taps * TAP_LANES), (16, taps * TAP_LANES)
    slots = {axis: EXTENT[axis] - 1 for axis in EXTENT}
    return [
        pltpu.VMEM((slots[first],) + one, jnp.bfloat16),
        pltpu.VMEM((slots[first],) + one, jnp.bfloat16),
        pltpu.VMEM(one, jnp.float32),
        pltpu.VMEM((slots["z"],) + two, jnp.bfloat16),
        pltpu.VMEM((slots["z"],) + two, jnp.bfloat16),
        pltpu.VMEM((EXTENT[third],) + two, jnp.bfloat16),
    ]


def greet(links):
    barrier = pltpu.get_barrier_semaphore()
    peers = [links.peer("z", shift) for shift in (1, -1, 2, -2, 3, -3)]
    peers += [links.beside(0, 1 - links.core)]
    peers += [links.peer(axis, shift) for axis in "xy" for shift in (1, -1, 2)]
    peers += [
        links.beside(shift, core) for shift in (1, -1) for core in (links.core, 1 - links.core)
    ]
    for device in peers:
        pl.semaphore_signal(
            barrier, inc=1, device_id=device, device_id_type=pl.DeviceIdType.MESH
        )
    pl.semaphore_wait(barrier, len(peers))


def shifted_copies(level, padded):
    channels = level.shape[3]
    along = lax.broadcasted_iota(jnp.int32, (RAD, AXIAL, channels), 1)
    rim = jnp.zeros((AXIAL, channels), jnp.bfloat16).astype(jnp.float32)

    def one_slab(slab, carry):
        here = level[1, slab].astype(jnp.float32).reshape(RAD, AXIAL, channels)
        below = jnp.where(along == 0, 0.0, pltpu.roll(here, 1, 1))
        above = jnp.where(along == AXIAL - 1, 0.0, pltpu.roll(here, AXIAL - 1, 1))
        for offset, values in ((0, below), (1, here), (2, above)):
            rows = values.reshape(ROWS, channels)
            if offset != 1:
                level[offset, slab] = rows.astype(jnp.bfloat16)
            padded[offset, slab] = jnp.concatenate((rim, rows, rim), axis=0).astype(jnp.bfloat16)
        return carry

    lax.fori_loop(0, AZ_DEV + 2, one_slab, 0)


def window(level, padded, along_az, along_rad, along_ax):
    channels = level.shape[3]
    slabs = pl.ds(along_az, AZ_DEV)
    if along_rad == 1:
        picked = level[along_ax, slabs]
    else:
        picked = padded[along_ax, slabs, pl.ds(AXIAL * along_rad, ROWS), :]
    return picked.reshape(CELLS_CHIP, channels)


def tap_lanes(along_az, along_rad, along_ax, width):
    tap = (along_az * 3 + along_rad) * 3 + along_ax
    start = tap * width
    return pl.ds(start if isinstance(tap, int) else pl.multiple_of(start, width), width)


def convolve_step(level, padded, weight, total, along_az, along_ax):
    added = total[...]
    for along_rad in range(3):
        added = added + lax.dot_general(
            window(level, padded, along_az, along_rad, along_ax),
            weight[:, tap_lanes(along_az, along_rad, along_ax, CH)],
            (((1,), (1,)), ((), ())),
            preferred_element_type=jnp.float32,
        )
    total[...] = added


def convolve(level, padded, weight, total):
    total[...] = jnp.zeros_like(total)

    def one_step(step, carry):
        convolve_step(level, padded, weight, total, step // 3, step % 3)
        return carry

    lax.fori_loop(0, 9, one_step, 0)


def convolve_back(level, padded, weight, total):
    total[...] = jnp.zeros_like(total)

    def one_step(step, carry):
        along_az, along_ax = step // 3, step % 3
        columns = jnp.concatenate(
            [window(level, padded, 2 - along_az, 2 - rad, 2 - along_ax) for rad in range(3)], axis=1
        )
        rows = jnp.concatenate(
            [weight[:, tap_lanes(along_az, rad, along_ax, CH)] for rad in range(3)], axis=0
        )
        update = jnp.dot(columns, rows, preferred_element_type=jnp.float32)
        for side in range(2):
            total[side] = total[side] + update[:, side * HALF : (side + 1) * HALF]
        return carry

    lax.fori_loop(0, 9, one_step, 0)


def weight_terms(turned, level, padded, terms, which, along_az):
    def one_step(along_ax, carry):
        for along_rad in range(3):
            update = jnp.dot(
                turned[...],
                window(level, padded, along_az, along_rad, along_ax),
                preferred_element_type=jnp.float32,
            )
            lanes = tap_lanes(along_az, along_rad, along_ax, HALF)
            for side in range(2):
                terms[2 * which + side, :, lanes] = update[:, side * HALF : (side + 1) * HALF]
        return carry

    lax.fori_loop(0, 3, one_step, 0)


def flow_part(links, features, level, padded, weight, total, mine, flow):
    core = links.core
    lanes = pl.ds(pl.multiple_of(core * HALF, HALF), HALF)
    total[...] = jnp.zeros_like(total)
    for step in range(9):
        yield None
        convolve_step(level, padded, weight, total, step // 3, step % 3)
        links.now += CONVOLVE_US
    own = features[1, pl.ds(1, AZ_DEV), :, lanes].astype(jnp.float32)
    mine[...] = (own + total[...].reshape(AZ_DEV, ROWS, HALF)).astype(jnp.bfloat16)
    here = pl.ds(pl.multiple_of(core * OWN_ROWS, OWN_ROWS), OWN_ROWS)
    there = pl.ds(pl.multiple_of((1 - core) * OWN_ROWS, OWN_ROWS), OWN_ROWS)
    flow[:, :, lanes] = mine[:, here, :]
    handle = links.send(mine.at[:, there, :], flow.at[:, :, lanes], links.beside(0, 1 - core))
    yield links.now + 60.0
    handle.wait_recv()


def exchange_rims(links, source, target, rows):
    core = links.core
    handles = []
    for to in (1 - core, core):
        for shift, slab, landing in ((1, AZ_DEV - 1, 0), (-1, 0, AZ_DEV + 1)):
            given, taken = source(slab, to), target(landing, to)
            handles.append(links.send(given, taken, links.beside(shift, to)))
        if to is not core:
            handles.append(
                links.send(
                    source(slice(None), to), target(pl.ds(1, AZ_DEV), to), links.beside(0, to)
                )
            )
    return handles


def whole_kernel(
    features,
    cotangent,
    w_first,
    w_second,
    flow,
    result,
    send_sems,
    recv_sems,
    local_sems,
    first_rows,
    second_rows,
    in_level,
    in_padded,
    cot_level,
    cot_padded,
    hid_level,
    hid_padded,
    pre,
    second,
    back,
    back_other,
    turned,
    mine,
    terms,
    *buffers,
):
    links = Links(send_sems, recv_sems)
    core = links.core
    here = pl.ds(pl.multiple_of(core * OWN_ROWS, OWN_ROWS), OWN_ROWS)
    cells = pl.ds(1, AZ_DEV)

    def lanes(which):
        return pl.ds(pl.multiple_of(which * HALF, HALF), HALF)

    loads = [
        pltpu.make_async_copy(*pair, local_sems.at[number])
        for number, pair in enumerate(
            (
                (features, in_level.at[1, cells, here, :]),
                (cotangent.at[:, :, lanes(core)], cot_level.at[1, cells, here, :]),
                (w_first, first_rows),
                (w_second, second_rows),
            )
        )
    ]
    for load in loads:
        load.start()
    greet(links)
    field_in = exchange_rims(
        links,
        lambda slab, to: features.at[slab],
        lambda slab, to: in_level.at[1, slab, here, :],
        here,
    )
    field_cot = exchange_rims(
        links,
        lambda slab, to: cotangent.at[slab, :, lanes(to)],
        lambda slab, to: cot_level.at[1, slab, here, :],
        here,
    )
    loads[0].wait()
    loads[2].wait()
    for handle in field_in:
        handle.wait_recv()
    shifted_copies(in_level, in_padded)
    convolve(in_level, in_padded, first_rows, pre)
    values = pre[...]
    hidden = values * jax.nn.sigmoid(values)
    hid_level[1, cells, :, lanes(core)] = hidden.astype(jnp.bfloat16).reshape(AZ_DEV, ROWS, HALF)
    field_hid = exchange_rims(
        links,
        lambda slab, to: hid_level.at[
            1, pl.ds(1, AZ_DEV) if isinstance(slab, slice) else slab + 1, :, lanes(core)
        ],
        lambda slab, to: hid_level.at[1, slab, :, lanes(core)],
        here,
    )
    loads[1].wait()
    loads[3].wait()
    for handle in field_cot:
        handle.wait_recv()
    shifted_copies(cot_level, cot_padded)
    convolve_back(cot_level, cot_padded, second_rows, back)
    swap = links.send(back.at[1 - core], back_other, links.beside(0, 1 - core))
    own_cot = cot_level[1, cells].reshape(CELLS_CHIP, HALF).astype(jnp.float32)
    turned[1] = own_cot.T.astype(jnp.bfloat16)
    swap.wait_recv()
    values = pre[...]
    sigma = jax.nn.sigmoid(values)
    slope = (back[core] + back_other[...]) * (sigma * (1.0 + values * (1.0 - sigma)))
    turned[0] = slope.T.astype(jnp.bfloat16)
    for along_az in range(3):
        weight_terms(turned.at[0], in_level, in_padded, terms, 0, along_az)
    for handle in field_hid:
        handle.wait_recv()
    shifted_copies(hid_level, hid_padded)
    waiting, used = [], 0

    def advance(one):
        links.now += STEP_US
        try:
            waiting.append((next(one), one))
        except StopIteration:
            pass

    for part in PARTS:
        if part[2] % 9 == 0:
            weight_terms(turned.at[1], hid_level, hid_padded, terms, 1, part[2] // 9)
            links.now += 1.0
        count = len(part_scratch(part))
        advance(reduce_part(links, part, terms, result, buffers[used : used + count]))
        used += count
    advance(flow_part(links, in_level, hid_level, hid_padded, second_rows, second, mine, flow))
    while waiting:
        due = [links.now + CONVOLVE_US if at is None else at for at, _ in waiting]
        soonest = min(range(len(due)), key=due.__getitem__)
        at, one = waiting.pop(soonest)
        links.now = max(links.now, at or 0.0)
        advance(one)
    for handle in links.started:
        handle.wait_send()


COPIES = 192


def whole_layer(features, cotangent, w_first, w_second):
    field = (3, AZ_DEV + 2, ROWS)
    padded = (3, AZ_DEV + 2, ROWS + 2 * AXIAL)
    scratch = [
        pltpu.SemaphoreType.DMA((COPIES,)),
        pltpu.SemaphoreType.DMA((COPIES,)),
        pltpu.SemaphoreType.DMA((4,)),
        pltpu.VMEM((HALF, TAPS * CH), jnp.bfloat16),
        pltpu.VMEM((HALF, TAPS * CH), jnp.bfloat16),
        pltpu.VMEM(field + (CH,), jnp.bfloat16),
        pltpu.VMEM(padded + (CH,), jnp.bfloat16),
        pltpu.VMEM(field + (HALF,), jnp.bfloat16),
        pltpu.VMEM(padded + (HALF,), jnp.bfloat16),
        pltpu.VMEM(field + (CH,), jnp.bfloat16),
        pltpu.VMEM(padded + (CH,), jnp.bfloat16),
        pltpu.VMEM((CELLS_CHIP, HALF), jnp.float32),
        pltpu.VMEM((CELLS_CHIP, HALF), jnp.float32),
        pltpu.VMEM((2, CELLS_CHIP, HALF), jnp.float32),
        pltpu.VMEM((CELLS_CHIP, HALF), jnp.float32),
        pltpu.VMEM((2, HALF, CELLS_CHIP), jnp.bfloat16),
        pltpu.VMEM((AZ_DEV, ROWS, HALF), jnp.bfloat16),
        pltpu.VMEM((4, HALF, TAPS * HALF), jnp.float32),
    ]
    for part in PARTS:
        scratch += part_scratch(part)
    return pl.pallas_call(
        whole_kernel,
        out_shape=(
            jax.ShapeDtypeStruct((AZ_DEV, OWN_ROWS, CH), jnp.bfloat16),
            jax.ShapeDtypeStruct((4, HALF, TAPS * HALF), jnp.bfloat16),
        ),
        in_specs=[pl.BlockSpec(memory_space=pl.ANY)] * 4,
        out_specs=(pl.BlockSpec(memory_space=pltpu.VMEM), pl.BlockSpec(memory_space=pltpu.VMEM)),
        scratch_shapes=scratch,
        compiler_params=pltpu.CompilerParams(
            collective_id=0, has_side_effects=True, vmem_limit_bytes=56 * 2**20
        ),
        name="both_layers",
    )(features, cotangent, w_first, w_second)


def widen_kernel(factor, summed, grad_first, grad_second):
    def put(target):
        for tap in range(9):
            for side in range(2):
                target[:, (2 * tap + side) * HALF : (2 * tap + side + 1) * HALF] = (
                    summed[side, :, tap * HALF : (tap + 1) * HALF].astype(jnp.float32) * factor
                )

    @pl.when(pl.program_id(0) == 0)
    def _():
        put(grad_first)

    @pl.when(pl.program_id(0) == 1)
    def _():
        put(grad_second)


def widen(summed, factor):
    third = TAPS * CH // 3
    shape = jax.ShapeDtypeStruct((HALF, TAPS * CH), jnp.float32)
    return pl.pallas_call(
        functools.partial(widen_kernel, factor),
        grid=(2, 3),
        out_shape=(shape, shape),
        in_specs=[pl.BlockSpec((2, HALF, third // 2), lambda g, p: (g, 0, p))],
        out_specs=(
            pl.BlockSpec((HALF, third), lambda g, p: (0, jnp.where(g == 0, p, 2))),
            pl.BlockSpec((HALF, third), lambda g, p: (0, jnp.where(g == 0, 0, p))),
        ),
        compiler_params=pltpu.CompilerParams(vmem_limit_bytes=24 * 2**20),
        name="widen",
    )(summed)


def local(features, cotangent, w_first, w_second):
    factor = 1.0 / math.sqrt(NX * NY * NZ * CELLS_CHIP)
    flow, summed = whole_layer(
        features.transpose(1, 2, 0), cotangent.transpose(1, 2, 0), w_first, w_second
    )
    grad_first, grad_second = widen(summed, factor)
    return (flow.transpose(2, 0, 1), grad_first, grad_second)


def solution(mesh):
    in_specs = (P(None, "az", "grp"), P(None, "az", "grp"), P("grp", None), P("grp", None))
    out_specs = (P(None, "az", "grp"), P("grp", None), P("grp", None))
    return jax.shard_map(local, mesh=mesh, in_specs=in_specs, out_specs=out_specs, check_vma=False)
```

```python
import functools
import math

import jax
import jax.numpy as jnp
from jax import lax
from jax.experimental import pallas as pl
from jax.experimental.pallas import tpu as pltpu
from jax.sharding import PartitionSpec as P

CH = 256
HALF = 128
TAPS = 27
RAD = 16
AXIAL = 8
AZ_DEV = 4
ROWS = RAD * AXIAL
OWN_ROWS = ROWS // 2
CELLS_CHIP = AZ_DEV * ROWS

NX, NY, NZ = 4, 4, 8
EXTENT = {"x": NX, "y": NY, "z": NZ}
TAP_LANES = 128
PARTS = (
    ((1,), "yzx", 0, 4, 1),
    ((1,), "yzx", 4, 6, -1),
    ((1,), "yzx", 10, 4, -1),
    ((1,), "xzy", 14, 4, 1),
    ((0,), "xzy", 0, 6, -1),
    ((0,), "xzy", 6, 6, 1),
    ((0,), "xzy", 12, 6, -1),
    ((0, 1), "yzx", 18, 3, 1),
    ((0, 1), "yzx", 21, 3, 1),
    ((0, 1), "zxy", 24, 3, -1),
)


BYTES_PER_US = 54000.0
SEND_US, HOP_US, STEP_US = 1.75, 0.3, 0.15
CONVOLVE_US, TERMS_US, SHIFT_US = 0.45, 1.0, 1.5


class Links:
    def __init__(self, send_sems, recv_sems):
        self.send_sems, self.recv_sems, self.used, self.started = send_sems, recv_sems, 0, []
        self.now, self.busy = 0.0, {}
        flat = lax.axis_index("az")
        self.flat, self.core = flat, lax.axis_index("grp")
        self.at = {"x": flat % NX, "y": (flat // NX) % NY, "z": flat // (NX * NY)}

    def index(self, axis, shift):
        return (self.at[axis] + (shift + EXTENT[axis])) % EXTENT[axis]

    def peer(self, axis, shift):
        to = dict(self.at)
        to[axis] = self.index(axis, shift)
        return {"az": (to["z"] * NY + to["y"]) * NX + to["x"], "grp": self.core}

    def beside(self, shift, core):
        count = NX * NY * NZ
        return {"az": (self.flat + (shift + count)) % count, "grp": core}

    def copy(self, source, target, axis, shift):
        lane, hops = (axis, shift > 0), abs(shift)
        begin = max(self.now, self.busy.get(lane, 0.0))
        self.busy[lane] = begin + hops * 2 * math.prod(source.shape) / BYTES_PER_US
        handle = self.send(source, target, self.peer(axis, shift))
        return handle, self.busy[lane] + SEND_US + HOP_US * hops

    def send(self, source, target, device):
        number = self.used
        self.used += 1
        handle = pltpu.make_async_remote_copy(
            src_ref=source,
            dst_ref=target,
            send_sem=self.send_sems.at[number],
            recv_sem=self.recv_sems.at[number],
            device_id=device,
            device_id_type=pl.DeviceIdType.MESH,
        )
        handle.start()
        self.started.append(handle)
        return handle


def piece(ref, part, axes, at):
    which, order, tap, taps, _ = part
    split = [axis for axis in order[:2] if axis != "z"][0]
    rows = pl.ds(pl.multiple_of(at["z"] * 16, 16), 16) if "z" in axes else slice(None)
    lanes = pl.ds(tap * TAP_LANES, taps * TAP_LANES)
    if split not in axes:
        return ref.at[pl.ds(2 * which[0], 2 * len(which)), rows, lanes]
    if len(which) == 2:
        return ref.at[at[split], rows, lanes]
    half = taps // 2
    begin = (tap + at[split] % 2 * half) * TAP_LANES
    lanes = pl.ds(pl.multiple_of(begin, TAP_LANES), half * TAP_LANES)
    return ref.at[2 * which[0] + at[split] // 2, rows, lanes]


ROUTES = {4: ((2, 1), (-1, -1)), 8: ((4, 1), (2, 1), (-3, -1), (-1, -1))}


def relays(axis):
    return [(owner - stop, stop) for owner, stop in ROUTES[EXTENT[axis]] if owner != stop]


def arrivals(axis):
    routes = ROUTES[EXTENT[axis]]
    return [onward for onward, _ in relays(axis)] + [o for o, stop in routes if o == stop]


def scatter_axis(links, axis, sense, own, stage, landing):
    first = []
    for slot, (owner, stop) in enumerate(ROUTES[EXTENT[axis]]):
        stage[slot] = own(links.index(axis, sense * owner)).astype(jnp.bfloat16)
        first.append(links.copy(stage.at[slot], landing.at[slot], axis, sense * stop))
    last = []
    slot = len(first)
    for number, (owner, stop) in enumerate(ROUTES[EXTENT[axis]]):
        handle, due = first[number]
        if owner == stop:
            last.append((number, handle, due))
            continue
        onward = owner - stop
        total = own(links.index(axis, sense * onward))
        yield due
        handle.wait_recv()
        stage[slot] = (total + landing[number].astype(jnp.float32)).astype(jnp.bfloat16)
        last.append((slot,) + links.copy(stage.at[slot], landing.at[slot], axis, sense * onward))
        slot += 1
    total = own(links.at[axis])
    yield max(due for _, _, due in last)
    for slot, handle, _ in last:
        handle.wait_recv()
        total = total + landing[slot].astype(jnp.float32)
    return total


def gather_axis(links, axis, sense, view):
    chunk = view(links.at[axis])
    first = [
        (onward,) + links.copy(chunk, chunk, axis, sense * onward) for onward in arrivals(axis)
    ]
    last = []
    for number, (onward, stop) in enumerate(relays(axis)):
        _, handle, due = first[number]
        yield due
        handle.wait_recv()
        chunk = view(links.index(axis, -sense * onward))
        last.append(links.copy(chunk, chunk, axis, sense * stop))
    last += [(handle, due) for _, handle, due in first[len(last) :]]
    yield max(due for _, due in last)
    for handle, _ in last:
        handle.wait_recv()


def reduce_part(links, part, source, result, buffers):
    which, (first, second, third), tap, taps, sense = part
    stage_one, landing_one, sum_one, stage_two, landing_two, landing_three = buffers
    at = links.at

    def own_first(index):
        return piece(source, part, (first,), {first: index})[...]

    sum_one[...] = yield from scatter_axis(
        links, first, sense, own_first, stage_one, landing_one
    )

    def own_second(index):
        if second == "z":
            return sum_one[pl.ds(pl.multiple_of(index * 16, 16), 16), :]
        return sum_one[index]

    total = yield from scatter_axis(links, second, -sense, own_second, stage_two, landing_two)
    mine = landing_three.at[at[third]]
    mine[...] = total.astype(jnp.bfloat16)
    sent = [links.copy(mine, mine, third, shift) for shift in (1, -1, 2)]
    yield max(due for _, due in sent)
    for handle, _ in sent:
        handle.wait_recv()
    total = landing_three[0].astype(jnp.float32)
    for index in range(1, EXTENT[third]):
        total = total + landing_three[index].astype(jnp.float32)
    both = (first, second)
    piece(result, part, both, at)[...] = total.astype(jnp.bfloat16)
    yield from gather_axis(
        links, second, sense, lambda index: piece(result, part, both, {**at, second: index})
    )
    yield from gather_axis(
        links, first, -sense, lambda index: piece(result, part, (first,), {first: index})
    )


def part_scratch(part):
    which, (first, second, third), tap, taps, sense = part
    lanes = taps * TAP_LANES * len(which) // 2
    two = (16, lanes)
    one = (4,) + two if first == "z" else (128, lanes)
    slots = {axis: EXTENT[axis] - 1 for axis in EXTENT}
    return [
        pltpu.VMEM((slots[first],) + one, jnp.bfloat16),
        pltpu.VMEM((slots[first],) + one, jnp.bfloat16),
        pltpu.VMEM(one, jnp.float32),
        pltpu.VMEM((slots[second],) + two, jnp.bfloat16),
        pltpu.VMEM((slots[second],) + two, jnp.bfloat16),
        pltpu.VMEM((EXTENT[third],) + two, jnp.bfloat16),
    ]


def greet(links):
    barrier = pltpu.get_barrier_semaphore()
    peers = [links.peer("z", shift) for shift in (1, -1, 2, -2, 3, -3)]
    peers += [links.beside(0, 1 - links.core)]
    peers += [links.peer(axis, shift) for axis in "xy" for shift in (1, -1, 2)]
    peers += [
        links.beside(shift, core) for shift in (1, -1) for core in (links.core, 1 - links.core)
    ]
    for device in peers:
        pl.semaphore_signal(
            barrier, inc=1, device_id=device, device_id_type=pl.DeviceIdType.MESH
        )
    pl.semaphore_wait(barrier, len(peers))


def shifted_copies(level, padded):
    channels = level.shape[3]
    along = lax.broadcasted_iota(jnp.int32, (RAD, AXIAL, channels), 1)
    rim = jnp.zeros((AXIAL, channels), jnp.bfloat16).astype(jnp.float32)

    def one_slab(slab, carry):
        here = level[1, slab].astype(jnp.float32).reshape(RAD, AXIAL, channels)
        below = jnp.where(along == 0, 0.0, pltpu.roll(here, 1, 1))
        above = jnp.where(along == AXIAL - 1, 0.0, pltpu.roll(here, AXIAL - 1, 1))
        for offset, values in ((0, below), (1, here), (2, above)):
            rows = values.reshape(ROWS, channels)
            if offset != 1:
                level[offset, slab] = rows.astype(jnp.bfloat16)
            padded[offset, slab] = jnp.concatenate((rim, rows, rim), axis=0).astype(jnp.bfloat16)
        return carry

    lax.fori_loop(0, AZ_DEV + 2, one_slab, 0)


def window(level, padded, along_az, along_rad, along_ax):
    channels = level.shape[3]
    slabs = pl.ds(along_az, AZ_DEV)
    if along_rad == 1:
        picked = level[along_ax, slabs]
    else:
        picked = padded[along_ax, slabs, pl.ds(AXIAL * along_rad, ROWS), :]
    return picked.reshape(CELLS_CHIP, channels)


def tap_lanes(along_az, along_rad, along_ax, width):
    tap = (along_az * 3 + along_rad) * 3 + along_ax
    start = tap * width
    return pl.ds(start if isinstance(tap, int) else pl.multiple_of(start, width), width)


def convolve_step(level, padded, weight, total, along_az, along_ax):
    added = total[...]
    for along_rad in range(3):
        added = added + lax.dot_general(
            window(level, padded, along_az, along_rad, along_ax),
            weight[:, tap_lanes(along_az, along_rad, along_ax, CH)],
            (((1,), (1,)), ((), ())),
            preferred_element_type=jnp.float32,
        )
    total[...] = added


def convolve(level, padded, weight, total):
    total[...] = jnp.zeros_like(total)

    def one_step(step, carry):
        convolve_step(level, padded, weight, total, step // 3, step % 3)
        return carry

    lax.fori_loop(0, 9, one_step, 0)


def convolve_back(level, padded, weight, total):
    total[...] = jnp.zeros_like(total)

    def one_step(step, carry):
        along_az, along_ax = step // 3, step % 3
        columns = jnp.concatenate(
            [window(level, padded, 2 - along_az, 2 - rad, 2 - along_ax) for rad in range(3)], axis=1
        )
        rows = jnp.concatenate(
            [weight[:, tap_lanes(along_az, rad, along_ax, CH)] for rad in range(3)], axis=0
        )
        update = jnp.dot(columns, rows, preferred_element_type=jnp.float32)
        for side in range(2):
            total[side] = total[side] + update[:, side * HALF : (side + 1) * HALF]
        return carry

    lax.fori_loop(0, 9, one_step, 0)


def weight_terms(turned, level, padded, terms, which, along_az):
    def one_step(along_ax, carry):
        for along_rad in range(3):
            update = jnp.dot(
                turned[...],
                window(level, padded, along_az, along_rad, along_ax),
                preferred_element_type=jnp.float32,
            )
            lanes = tap_lanes(along_az, along_rad, along_ax, HALF)
            for side in range(2):
                terms[2 * which + side, :, lanes] = update[:, side * HALF : (side + 1) * HALF]
        return carry

    lax.fori_loop(0, 3, one_step, 0)


def flow_part(links, features, level, padded, weight, total, mine, flow):
    core = links.core
    lanes = pl.ds(pl.multiple_of(core * HALF, HALF), HALF)
    total[...] = jnp.zeros_like(total)
    for step in range(9):
        yield None
        convolve_step(level, padded, weight, total, step // 3, step % 3)
        links.now += CONVOLVE_US
    own = features[1, pl.ds(1, AZ_DEV), :, lanes].astype(jnp.float32)
    mine[...] = (own + total[...].reshape(AZ_DEV, ROWS, HALF)).astype(jnp.bfloat16)
    here = pl.ds(pl.multiple_of(core * OWN_ROWS, OWN_ROWS), OWN_ROWS)
    there = pl.ds(pl.multiple_of((1 - core) * OWN_ROWS, OWN_ROWS), OWN_ROWS)
    flow[:, :, lanes] = mine[:, here, :]
    handle = links.send(mine.at[:, there, :], flow.at[:, :, lanes], links.beside(0, 1 - core))
    yield links.now + 60.0
    handle.wait_recv()


def exchange_rims(links, source, target, rows):
    core = links.core
    handles = []
    for to in (1 - core, core):
        for shift, slab, landing in ((1, AZ_DEV - 1, 0), (-1, 0, AZ_DEV + 1)):
            given, taken = source(slab, to), target(landing, to)
            handles.append(links.send(given, taken, links.beside(shift, to)))
        if to is not core:
            handles.append(
                links.send(
                    source(slice(None), to), target(pl.ds(1, AZ_DEV), to), links.beside(0, to)
                )
            )
    return handles


def whole_kernel(
    features,
    cotangent,
    w_first,
    w_second,
    flow,
    result,
    send_sems,
    recv_sems,
    local_sems,
    first_rows,
    second_rows,
    in_level,
    in_padded,
    cot_level,
    cot_padded,
    hid_level,
    hid_padded,
    pre,
    second,
    back,
    back_other,
    turned,
    mine,
    terms,
    held,
    *buffers,
):
    links = Links(send_sems, recv_sems)
    core = links.core
    here = pl.ds(pl.multiple_of(core * OWN_ROWS, OWN_ROWS), OWN_ROWS)
    cells = pl.ds(1, AZ_DEV)

    def lanes(which):
        return pl.ds(pl.multiple_of(which * HALF, HALF), HALF)

    loads = [
        pltpu.make_async_copy(*pair, local_sems.at[number])
        for number, pair in enumerate(
            (
                (features, in_level.at[1, cells, here, :]),
                (cotangent.at[:, :, lanes(core)], cot_level.at[1, cells, here, :]),
                (w_first, first_rows),
                (w_second, second_rows),
            )
        )
    ]
    for load in loads:
        load.start()
    greet(links)
    field_in = exchange_rims(
        links,
        lambda slab, to: features.at[slab],
        lambda slab, to: in_level.at[1, slab, here, :],
        here,
    )
    field_cot = exchange_rims(
        links,
        lambda slab, to: cotangent.at[slab, :, lanes(to)],
        lambda slab, to: cot_level.at[1, slab, here, :],
        here,
    )
    loads[0].wait()
    loads[2].wait()
    for handle in field_in:
        handle.wait_recv()
    shifted_copies(in_level, in_padded)
    convolve(in_level, in_padded, first_rows, pre)
    values = pre[...]
    hidden = values * jax.nn.sigmoid(values)
    hid_level[1, cells, :, lanes(core)] = hidden.astype(jnp.bfloat16).reshape(AZ_DEV, ROWS, HALF)
    field_hid = exchange_rims(
        links,
        lambda slab, to: hid_level.at[
            1, pl.ds(1, AZ_DEV) if isinstance(slab, slice) else slab + 1, :, lanes(core)
        ],
        lambda slab, to: hid_level.at[1, slab, :, lanes(core)],
        here,
    )
    loads[1].wait()
    loads[3].wait()
    for handle in field_cot:
        handle.wait_recv()
    shifted_copies(cot_level, cot_padded)
    convolve_back(cot_level, cot_padded, second_rows, back)
    swap = links.send(back.at[1 - core], back_other, links.beside(0, 1 - core))
    own_cot = cot_level[1, cells].reshape(CELLS_CHIP, HALF).astype(jnp.float32)
    turned[1] = own_cot.T.astype(jnp.bfloat16)
    for handle in field_hid:
        handle.wait_recv()
    shifted_copies(hid_level, hid_padded)
    parts, used = [], 0
    for part in PARTS:
        count = len(part_scratch(part))
        parts.append((part, buffers[used : used + count]))
        used += count
    stored = []

    def one_part(part, scratch):
        yield from reduce_part(links, part, terms, held, scratch)
        done = [piece(ref, part, (), {}) for ref in (held, result)]
        stored.append(pltpu.make_async_copy(*done, local_sems.at[4 + len(stored)]))
        stored[-1].start()

    def gradients():
        ready = set()
        for which in (1, 0):
            if which == 0:
                swap.wait_recv()
                values = pre[...]
                sigma = jax.nn.sigmoid(values)
                slope = (back[core] + back_other[...]) * (sigma * (1.0 + values * (1.0 - sigma)))
                turned[0] = slope.T.astype(jnp.bfloat16)
            level, padded = (in_level, in_padded) if which == 0 else (hid_level, hid_padded)
            for along_az in range(3):
                weight_terms(turned.at[which], level, padded, terms, which, along_az)
                links.now += TERMS_US
                ready |= {(which, 9 * along_az + tap) for tap in range(9)}
                for one in list(parts):
                    grads, _, tap, taps, _ = one[0]
                    if {(g, t) for g in grads for t in range(tap, tap + taps)} <= ready:
                        parts.remove(one)
                        advance(one_part(*one))
                yield 0.0
        advance(flow_part(links, in_level, hid_level, hid_padded, second_rows, second, mine, flow))

    waiting = []

    def advance(one):
        links.now += STEP_US
        try:
            waiting.append((next(one), one))
        except StopIteration:
            pass

    advance(gradients())
    while waiting:
        due = [links.now + CONVOLVE_US if at is None else at or links.now for at, _ in waiting]
        soonest = min(range(len(due)), key=due.__getitem__)
        at, one = waiting.pop(soonest)
        links.now = max(links.now, at or 0.0)
        advance(one)
    for copy in stored:
        copy.wait()
    for handle in links.started:
        handle.wait_send()


COPIES = 256


def whole_layer(features, cotangent, w_first, w_second):
    field = (3, AZ_DEV + 2, ROWS)
    padded = (3, AZ_DEV + 2, ROWS + 2 * AXIAL)
    scratch = [
        pltpu.SemaphoreType.DMA((COPIES,)),
        pltpu.SemaphoreType.DMA((COPIES,)),
        pltpu.SemaphoreType.DMA((4 + len(PARTS),)),
        pltpu.VMEM((HALF, TAPS * CH), jnp.bfloat16),
        pltpu.VMEM((HALF, TAPS * CH), jnp.bfloat16),
        pltpu.VMEM(field + (CH,), jnp.bfloat16),
        pltpu.VMEM(padded + (CH,), jnp.bfloat16),
        pltpu.VMEM(field + (HALF,), jnp.bfloat16),
        pltpu.VMEM(padded + (HALF,), jnp.bfloat16),
        pltpu.VMEM(field + (CH,), jnp.bfloat16),
        pltpu.VMEM(padded + (CH,), jnp.bfloat16),
        pltpu.VMEM((CELLS_CHIP, HALF), jnp.float32),
        pltpu.VMEM((CELLS_CHIP, HALF), jnp.float32),
        pltpu.VMEM((2, CELLS_CHIP, HALF), jnp.float32),
        pltpu.VMEM((CELLS_CHIP, HALF), jnp.float32),
        pltpu.VMEM((2, HALF, CELLS_CHIP), jnp.bfloat16),
        pltpu.VMEM((AZ_DEV, ROWS, HALF), jnp.bfloat16),
        pltpu.VMEM((4, HALF, TAPS * HALF), jnp.float32),
        pltpu.VMEM((4, HALF, TAPS * HALF), jnp.bfloat16),
    ]
    for part in PARTS:
        scratch += part_scratch(part)
    return pl.pallas_call(
        whole_kernel,
        out_shape=(
            jax.ShapeDtypeStruct((AZ_DEV, OWN_ROWS, CH), jnp.bfloat16),
            jax.ShapeDtypeStruct((4, HALF, TAPS * HALF), jnp.bfloat16),
        ),
        in_specs=[pl.BlockSpec(memory_space=pl.ANY)] * 4,
        out_specs=(pl.BlockSpec(memory_space=pltpu.VMEM), pl.BlockSpec(memory_space=pl.ANY)),
        scratch_shapes=scratch,
        compiler_params=pltpu.CompilerParams(
            collective_id=0, has_side_effects=True, vmem_limit_bytes=56 * 2**20
        ),
        name="both_layers",
    )(features, cotangent, w_first, w_second)


def widen_kernel(factor, summed, grad_first, grad_second):
    def put(target):
        for tap in range(9):
            for side in range(2):
                target[:, (2 * tap + side) * HALF : (2 * tap + side + 1) * HALF] = (
                    summed[side, :, tap * HALF : (tap + 1) * HALF].astype(jnp.float32) * factor
                )

    @pl.when(pl.program_id(0) == 0)
    def _():
        put(grad_first)

    @pl.when(pl.program_id(0) == 1)
    def _():
        put(grad_second)


def widen(summed, factor):
    third = TAPS * CH // 3
    shape = jax.ShapeDtypeStruct((HALF, TAPS * CH), jnp.float32)
    return pl.pallas_call(
        functools.partial(widen_kernel, factor),
        grid=(2, 3),
        out_shape=(shape, shape),
        in_specs=[pl.BlockSpec((2, HALF, third // 2), lambda g, p: (g, 0, p))],
        out_specs=(
            pl.BlockSpec((HALF, third), lambda g, p: (0, jnp.where(g == 0, p, 2))),
            pl.BlockSpec((HALF, third), lambda g, p: (0, jnp.where(g == 0, 0, p))),
        ),
        compiler_params=pltpu.CompilerParams(vmem_limit_bytes=60 * 2**20),
        name="widen",
    )(summed)


def local(features, cotangent, w_first, w_second):
    factor = 1.0 / math.sqrt(NX * NY * NZ * CELLS_CHIP)
    flow, summed = whole_layer(
        features.transpose(1, 2, 0), cotangent.transpose(1, 2, 0), w_first, w_second
    )
    grad_first, grad_second = widen(summed, factor)
    return (flow.transpose(2, 0, 1), grad_first, grad_second)


def solution(mesh):
    in_specs = (P(None, "az", "grp"), P(None, "az", "grp"), P("grp", None), P("grp", None))
    out_specs = (P(None, "az", "grp"), P("grp", None), P("grp", None))
    return jax.shard_map(local, mesh=mesh, in_specs=in_specs, out_specs=out_specs, check_vma=False)
```

```python
import functools
import math

import jax
import jax.numpy as jnp
from jax import lax
from jax.experimental import pallas as pl
from jax.experimental.pallas import tpu as pltpu
from jax.sharding import PartitionSpec as P

CH = 256
HALF = 128
TAPS = 27
RAD = 16
AXIAL = 8
AZ_DEV = 4
ROWS = RAD * AXIAL
OWN_ROWS = ROWS // 2
CELLS_CHIP = AZ_DEV * ROWS

NX, NY, NZ = 4, 4, 8
EXTENT = {"x": NX, "y": NY, "z": NZ}
TAP_LANES = 128
PARTS = (
    ((1,), "yzx", 0, 2, 1),
    ((1,), "xzy", 2, 4, 1),
    ((1,), "xzy", 6, 6, -1),
    ((1,), "yzx", 12, 6, 1),
    ((0,), "xzy", 0, 6, 1),
    ((0,), "xzy", 6, 6, -1),
    ((0,), "yzx", 12, 6, -1),
    ((0, 1), "yzx", 18, 3, 1),
    ((0, 1), "yzx", 21, 3, 1),
    ((0, 1), "xzy", 24, 3, 1),
)


BYTES_PER_US = 54000.0
SEND_US, HOP_US, STEP_US = 1.75, 0.3, 0.15
CONVOLVE_US, TERMS_US, SHIFT_US = 0.45, 1.0, 1.5


class Links:
    def __init__(self, send_sems, recv_sems):
        self.send_sems, self.recv_sems, self.used, self.started = send_sems, recv_sems, 0, []
        self.now, self.busy = 0.0, {}
        flat = lax.axis_index("az")
        self.flat, self.core = flat, lax.axis_index("grp")
        self.at = {"x": flat % NX, "y": (flat // NX) % NY, "z": flat // (NX * NY)}

    def index(self, axis, shift):
        return (self.at[axis] + (shift + EXTENT[axis])) % EXTENT[axis]

    def peer(self, axis, shift):
        to = dict(self.at)
        to[axis] = self.index(axis, shift)
        return {"az": (to["z"] * NY + to["y"]) * NX + to["x"], "grp": self.core}

    def beside(self, shift, core):
        count = NX * NY * NZ
        return {"az": (self.flat + (shift + count)) % count, "grp": core}

    def copy(self, source, target, axis, shift):
        lane, hops = (axis, shift > 0), abs(shift)
        begin = max(self.now, self.busy.get(lane, 0.0))
        self.busy[lane] = begin + hops * 2 * math.prod(source.shape) / BYTES_PER_US
        handle = self.send(source, target, self.peer(axis, shift))
        return handle, self.busy[lane] + SEND_US + HOP_US * hops

    def send(self, source, target, device):
        number = self.used
        self.used += 1
        handle = pltpu.make_async_remote_copy(
            src_ref=source,
            dst_ref=target,
            send_sem=self.send_sems.at[number],
            recv_sem=self.recv_sems.at[number],
            device_id=device,
            device_id_type=pl.DeviceIdType.MESH,
        )
        handle.start()
        self.started.append(handle)
        return handle


def piece(ref, part, axes, at):
    which, order, tap, taps, _ = part
    split = [axis for axis in order[:2] if axis != "z"][0]
    rows = pl.ds(pl.multiple_of(at["z"] * 16, 16), 16) if "z" in axes else slice(None)
    lanes = pl.ds(tap * TAP_LANES, taps * TAP_LANES)
    if split not in axes:
        return ref.at[pl.ds(2 * which[0], 2 * len(which)), rows, lanes]
    if len(which) == 2:
        return ref.at[at[split], rows, lanes]
    half = taps // 2
    begin = (tap + at[split] % 2 * half) * TAP_LANES
    lanes = pl.ds(pl.multiple_of(begin, TAP_LANES), half * TAP_LANES)
    return ref.at[2 * which[0] + at[split] // 2, rows, lanes]


ROUTES = {4: ((2, 1), (-1, -1)), 8: ((4, 1), (2, 1), (-3, -1), (-1, -1))}


def relays(axis):
    return [(owner - stop, stop) for owner, stop in ROUTES[EXTENT[axis]] if owner != stop]


def arrivals(axis):
    routes = ROUTES[EXTENT[axis]]
    return [onward for onward, _ in relays(axis)] + [o for o, stop in routes if o == stop]


def scatter_axis(links, axis, sense, own, stage, landing):
    first = []
    for slot, (owner, stop) in enumerate(ROUTES[EXTENT[axis]]):
        stage[slot] = own(links.index(axis, sense * owner)).astype(jnp.bfloat16)
        first.append(links.copy(stage.at[slot], landing.at[slot], axis, sense * stop))
    last = []
    slot = len(first)
    for number, (owner, stop) in enumerate(ROUTES[EXTENT[axis]]):
        handle, due = first[number]
        if owner == stop:
            last.append((number, handle, due))
            continue
        onward = owner - stop
        total = own(links.index(axis, sense * onward))
        yield due
        handle.wait_recv()
        stage[slot] = (total + landing[number].astype(jnp.float32)).astype(jnp.bfloat16)
        last.append((slot,) + links.copy(stage.at[slot], landing.at[slot], axis, sense * onward))
        slot += 1
    total = own(links.at[axis])
    yield max(due for _, _, due in last)
    for slot, handle, _ in last:
        handle.wait_recv()
        total = total + landing[slot].astype(jnp.float32)
    return total


def gather_axis(links, axis, sense, view):
    chunk = view(links.at[axis])
    first = [
        (onward,) + links.copy(chunk, chunk, axis, sense * onward) for onward in arrivals(axis)
    ]
    last = []
    for number, (onward, stop) in enumerate(relays(axis)):
        _, handle, due = first[number]
        yield due
        handle.wait_recv()
        chunk = view(links.index(axis, -sense * onward))
        last.append(links.copy(chunk, chunk, axis, sense * stop))
    last += [(handle, due) for _, handle, due in first[len(last) :]]
    yield max(due for _, due in last)
    for handle, _ in last:
        handle.wait_recv()


def reduce_part(links, part, source, result, buffers):
    which, (first, second, third), tap, taps, sense = part
    stage_one, landing_one, sum_one, stage_two, landing_two, landing_three = buffers
    at = links.at

    def own_first(index):
        return piece(source, part, (first,), {first: index})[...]

    sum_one[...] = yield from scatter_axis(
        links, first, sense, own_first, stage_one, landing_one
    )

    def own_second(index):
        if second == "z":
            return sum_one[pl.ds(pl.multiple_of(index * 16, 16), 16), :]
        return sum_one[index]

    total = yield from scatter_axis(links, second, -sense, own_second, stage_two, landing_two)
    mine = landing_three.at[at[third]]
    mine[...] = total.astype(jnp.bfloat16)
    sent = [links.copy(mine, mine, third, shift) for shift in (1, -1, 2)]
    yield max(due for _, due in sent)
    for handle, _ in sent:
        handle.wait_recv()
    total = landing_three[0].astype(jnp.float32)
    for index in range(1, EXTENT[third]):
        total = total + landing_three[index].astype(jnp.float32)
    both = (first, second)
    piece(result, part, both, at)[...] = total.astype(jnp.bfloat16)
    yield from gather_axis(
        links, second, sense, lambda index: piece(result, part, both, {**at, second: index})
    )
    yield from gather_axis(
        links, first, -sense, lambda index: piece(result, part, (first,), {first: index})
    )


def part_scratch(part):
    which, (first, second, third), tap, taps, sense = part
    lanes = taps * TAP_LANES * len(which) // 2
    two = (16, lanes)
    one = (4,) + two if first == "z" else (128, lanes)
    slots = {axis: EXTENT[axis] - 1 for axis in EXTENT}
    return [
        pltpu.VMEM((slots[first],) + one, jnp.bfloat16),
        pltpu.VMEM((slots[first],) + one, jnp.bfloat16),
        pltpu.VMEM(one, jnp.float32),
        pltpu.VMEM((slots[second],) + two, jnp.bfloat16),
        pltpu.VMEM((slots[second],) + two, jnp.bfloat16),
        pltpu.VMEM((EXTENT[third],) + two, jnp.bfloat16),
    ]


def greet(links):
    barrier = pltpu.get_barrier_semaphore()
    peers = [links.peer("z", shift) for shift in (1, -1, 2, -2, 3, -3)]
    peers += [links.beside(0, 1 - links.core)]
    peers += [links.peer(axis, shift) for axis in "xy" for shift in (1, -1, 2)]
    peers += [
        links.beside(shift, core) for shift in (1, -1) for core in (links.core, 1 - links.core)
    ]
    for device in peers:
        pl.semaphore_signal(
            barrier, inc=1, device_id=device, device_id_type=pl.DeviceIdType.MESH
        )
    pl.semaphore_wait(barrier, len(peers))


def shifted_copies(level, padded):
    channels = level.shape[3]
    along = lax.broadcasted_iota(jnp.int32, (RAD, AXIAL, channels), 1)
    rim = jnp.zeros((AXIAL, channels), jnp.bfloat16).astype(jnp.float32)

    def one_slab(slab, carry):
        here = level[1, slab].astype(jnp.float32).reshape(RAD, AXIAL, channels)
        below = jnp.where(along == 0, 0.0, pltpu.roll(here, 1, 1))
        above = jnp.where(along == AXIAL - 1, 0.0, pltpu.roll(here, AXIAL - 1, 1))
        for offset, values in ((0, below), (1, here), (2, above)):
            rows = values.reshape(ROWS, channels)
            if offset != 1:
                level[offset, slab] = rows.astype(jnp.bfloat16)
            padded[offset, slab] = jnp.concatenate((rim, rows, rim), axis=0).astype(jnp.bfloat16)
        return carry

    lax.fori_loop(0, AZ_DEV + 2, one_slab, 0)


def window(level, padded, along_az, along_rad, along_ax):
    channels = level.shape[3]
    slabs = pl.ds(along_az, AZ_DEV)
    if along_rad == 1:
        picked = level[along_ax, slabs]
    else:
        picked = padded[along_ax, slabs, pl.ds(AXIAL * along_rad, ROWS), :]
    return picked.reshape(CELLS_CHIP, channels)


def tap_lanes(along_az, along_rad, along_ax, width):
    tap = (along_az * 3 + along_rad) * 3 + along_ax
    start = tap * width
    return pl.ds(start if isinstance(tap, int) else pl.multiple_of(start, width), width)


def convolve_step(level, padded, weight, total, along_az, along_ax):
    added = total[...]
    for along_rad in range(3):
        added = added + lax.dot_general(
            window(level, padded, along_az, along_rad, along_ax),
            weight[:, tap_lanes(along_az, along_rad, along_ax, CH)],
            (((1,), (1,)), ((), ())),
            preferred_element_type=jnp.float32,
        )
    total[...] = added


def convolve(level, padded, weight, total):
    total[...] = jnp.zeros_like(total)

    def one_step(step, carry):
        convolve_step(level, padded, weight, total, step // 3, step % 3)
        return carry

    lax.fori_loop(0, 9, one_step, 0)


def convolve_back(level, padded, weight, total):
    total[...] = jnp.zeros_like(total)

    def one_step(step, carry):
        along_az, along_ax = step // 3, step % 3
        columns = jnp.concatenate(
            [window(level, padded, 2 - along_az, 2 - rad, 2 - along_ax) for rad in range(3)], axis=1
        )
        rows = jnp.concatenate(
            [weight[:, tap_lanes(along_az, rad, along_ax, CH)] for rad in range(3)], axis=0
        )
        update = jnp.dot(columns, rows, preferred_element_type=jnp.float32)
        for side in range(2):
            total[side] = total[side] + update[:, side * HALF : (side + 1) * HALF]
        return carry

    lax.fori_loop(0, 9, one_step, 0)


def weight_terms(turned, level, padded, terms, which, along_az):
    def one_step(along_ax, carry):
        for along_rad in range(3):
            update = jnp.dot(
                turned[...],
                window(level, padded, along_az, along_rad, along_ax),
                preferred_element_type=jnp.float32,
            )
            lanes = tap_lanes(along_az, along_rad, along_ax, HALF)
            for side in range(2):
                terms[2 * which + side, :, lanes] = update[:, side * HALF : (side + 1) * HALF]
        return carry

    lax.fori_loop(0, 3, one_step, 0)


def flow_part(links, features, level, padded, weight, total, mine, flow):
    core = links.core
    lanes = pl.ds(pl.multiple_of(core * HALF, HALF), HALF)
    total[...] = jnp.zeros_like(total)
    for step in range(9):
        yield None
        convolve_step(level, padded, weight, total, step // 3, step % 3)
        links.now += CONVOLVE_US
    own = features[1, pl.ds(1, AZ_DEV), :, lanes].astype(jnp.float32)
    mine[...] = (own + total[...].reshape(AZ_DEV, ROWS, HALF)).astype(jnp.bfloat16)
    here = pl.ds(pl.multiple_of(core * OWN_ROWS, OWN_ROWS), OWN_ROWS)
    there = pl.ds(pl.multiple_of((1 - core) * OWN_ROWS, OWN_ROWS), OWN_ROWS)
    flow[:, :, lanes] = mine[:, here, :]
    handle = links.send(mine.at[:, there, :], flow.at[:, :, lanes], links.beside(0, 1 - core))
    yield links.now + 60.0
    handle.wait_recv()


def exchange_rims(links, source, target, rows):
    core = links.core
    handles = []
    for to in (1 - core, core):
        for shift, slab, landing in ((1, AZ_DEV - 1, 0), (-1, 0, AZ_DEV + 1)):
            given, taken = source(slab, to), target(landing, to)
            handles.append(links.send(given, taken, links.beside(shift, to)))
        if to is not core:
            handles.append(
                links.send(
                    source(slice(None), to), target(pl.ds(1, AZ_DEV), to), links.beside(0, to)
                )
            )
    return handles


def whole_kernel(
    features,
    cotangent,
    w_first,
    w_second,
    flow,
    result,
    send_sems,
    recv_sems,
    local_sems,
    first_rows,
    second_rows,
    in_level,
    in_padded,
    cot_level,
    cot_padded,
    hid_level,
    hid_padded,
    pre,
    second,
    back,
    back_other,
    turned,
    mine,
    terms,
    held,
    *buffers,
):
    links = Links(send_sems, recv_sems)
    core = links.core
    here = pl.ds(pl.multiple_of(core * OWN_ROWS, OWN_ROWS), OWN_ROWS)
    cells = pl.ds(1, AZ_DEV)

    def lanes(which):
        return pl.ds(pl.multiple_of(which * HALF, HALF), HALF)

    loads = [
        pltpu.make_async_copy(*pair, local_sems.at[number])
        for number, pair in enumerate(
            (
                (features, in_level.at[1, cells, here, :]),
                (cotangent.at[:, :, lanes(core)], cot_level.at[1, cells, here, :]),
                (w_first, first_rows),
                (w_second, second_rows),
            )
        )
    ]
    for load in loads:
        load.start()
    greet(links)
    field_in = exchange_rims(
        links,
        lambda slab, to: features.at[slab],
        lambda slab, to: in_level.at[1, slab, here, :],
        here,
    )
    field_cot = exchange_rims(
        links,
        lambda slab, to: cotangent.at[slab, :, lanes(to)],
        lambda slab, to: cot_level.at[1, slab, here, :],
        here,
    )
    loads[0].wait()
    loads[2].wait()
    for handle in field_in:
        handle.wait_recv()
    shifted_copies(in_level, in_padded)
    convolve(in_level, in_padded, first_rows, pre)
    values = pre[...]
    hidden = values * jax.nn.sigmoid(values)
    hid_level[1, cells, :, lanes(core)] = hidden.astype(jnp.bfloat16).reshape(AZ_DEV, ROWS, HALF)
    field_hid = exchange_rims(
        links,
        lambda slab, to: hid_level.at[
            1, pl.ds(1, AZ_DEV) if isinstance(slab, slice) else slab + 1, :, lanes(core)
        ],
        lambda slab, to: hid_level.at[1, slab, :, lanes(core)],
        here,
    )
    loads[1].wait()
    loads[3].wait()
    for handle in field_cot:
        handle.wait_recv()
    shifted_copies(cot_level, cot_padded)
    convolve_back(cot_level, cot_padded, second_rows, back)
    swap = links.send(back.at[1 - core], back_other, links.beside(0, 1 - core))
    own_cot = cot_level[1, cells].reshape(CELLS_CHIP, HALF).astype(jnp.float32)
    turned[1] = own_cot.T.astype(jnp.bfloat16)
    for handle in field_hid:
        handle.wait_recv()
    shifted_copies(hid_level, hid_padded)
    parts, used = [], 0
    for part in PARTS:
        count = len(part_scratch(part))
        parts.append((part, buffers[used : used + count]))
        used += count
    stored = []

    def one_part(part, scratch):
        yield from reduce_part(links, part, terms, held, scratch)
        done = [piece(ref, part, (), {}) for ref in (held, result)]
        stored.append(pltpu.make_async_copy(*done, local_sems.at[4 + len(stored)]))
        stored[-1].start()

    def gradients():
        ready = set()
        for which in (1, 0):
            if which == 0:
                swap.wait_recv()
                values = pre[...]
                sigma = jax.nn.sigmoid(values)
                slope = (back[core] + back_other[...]) * (sigma * (1.0 + values * (1.0 - sigma)))
                turned[0] = slope.T.astype(jnp.bfloat16)
            level, padded = (in_level, in_padded) if which == 0 else (hid_level, hid_padded)
            for along_az in range(3):
                weight_terms(turned.at[which], level, padded, terms, which, along_az)
                links.now += TERMS_US
                ready |= {(which, 9 * along_az + tap) for tap in range(9)}
                for one in list(parts):
                    grads, _, tap, taps, _ = one[0]
                    if {(g, t) for g in grads for t in range(tap, tap + taps)} <= ready:
                        parts.remove(one)
                        advance(one_part(*one))
                yield 0.0
        advance(flow_part(links, in_level, hid_level, hid_padded, second_rows, second, mine, flow))

    waiting = []

    def advance(one):
        links.now += STEP_US
        try:
            waiting.append((next(one), one))
        except StopIteration:
            pass

    advance(gradients())
    while waiting:
        due = [links.now + CONVOLVE_US if at is None else at or links.now for at, _ in waiting]
        soonest = min(range(len(due)), key=due.__getitem__)
        at, one = waiting.pop(soonest)
        links.now = max(links.now, at or 0.0)
        advance(one)
    for copy in stored:
        copy.wait()
    for handle in links.started:
        handle.wait_send()


COPIES = 256


def whole_layer(features, cotangent, w_first, w_second):
    field = (3, AZ_DEV + 2, ROWS)
    padded = (3, AZ_DEV + 2, ROWS + 2 * AXIAL)
    scratch = [
        pltpu.SemaphoreType.DMA((COPIES,)),
        pltpu.SemaphoreType.DMA((COPIES,)),
        pltpu.SemaphoreType.DMA((4 + len(PARTS),)),
        pltpu.VMEM((HALF, TAPS * CH), jnp.bfloat16),
        pltpu.VMEM((HALF, TAPS * CH), jnp.bfloat16),
        pltpu.VMEM(field + (CH,), jnp.bfloat16),
        pltpu.VMEM(padded + (CH,), jnp.bfloat16),
        pltpu.VMEM(field + (HALF,), jnp.bfloat16),
        pltpu.VMEM(padded + (HALF,), jnp.bfloat16),
        pltpu.VMEM(field + (CH,), jnp.bfloat16),
        pltpu.VMEM(padded + (CH,), jnp.bfloat16),
        pltpu.VMEM((CELLS_CHIP, HALF), jnp.float32),
        pltpu.VMEM((CELLS_CHIP, HALF), jnp.float32),
        pltpu.VMEM((2, CELLS_CHIP, HALF), jnp.float32),
        pltpu.VMEM((CELLS_CHIP, HALF), jnp.float32),
        pltpu.VMEM((2, HALF, CELLS_CHIP), jnp.bfloat16),
        pltpu.VMEM((AZ_DEV, ROWS, HALF), jnp.bfloat16),
        pltpu.VMEM((4, HALF, TAPS * HALF), jnp.float32),
        pltpu.VMEM((4, HALF, TAPS * HALF), jnp.bfloat16),
    ]
    for part in PARTS:
        scratch += part_scratch(part)
    return pl.pallas_call(
        whole_kernel,
        out_shape=(
            jax.ShapeDtypeStruct((AZ_DEV, OWN_ROWS, CH), jnp.bfloat16),
            jax.ShapeDtypeStruct((4, HALF, TAPS * HALF), jnp.bfloat16),
        ),
        in_specs=[pl.BlockSpec(memory_space=pltpu.HBM)] * 4,
        out_specs=(pl.BlockSpec(memory_space=pltpu.VMEM), pl.BlockSpec(memory_space=pl.ANY)),
        scratch_shapes=scratch,
        compiler_params=pltpu.CompilerParams(
            collective_id=0, has_side_effects=True, vmem_limit_bytes=56 * 2**20
        ),
        name="both_layers",
    )(features, cotangent, w_first, w_second)


def widen_kernel(factor, summed, grad_first, grad_second, taken, wide, in_sems, out_sems):
    pieces = [(which, third) for which in range(2) for third in range(3)]
    loads, stores = [], []
    for number, (which, third) in enumerate(pieces):
        view = (pl.ds(2 * which, 2), slice(None), pl.ds(third * 9 * HALF, 9 * HALF))
        loads.append(
            pltpu.make_async_copy(summed.at[view], taken.at[view], in_sems.at[number])
        )
        loads[-1].start()
    for number, (which, third) in enumerate(pieces):
        loads[number].wait()
        for tap in range(9 * third, 9 * third + 9):
            for side in range(2):
                wide[which, :, (2 * tap + side) * HALF : (2 * tap + side + 1) * HALF] = (
                    taken[2 * which + side, :, tap * HALF : (tap + 1) * HALF].astype(jnp.float32)
                    * factor
                )
        view = (slice(None), pl.ds(third * 9 * CH, 9 * CH))
        target = grad_second if which else grad_first
        stores.append(
            pltpu.make_async_copy(wide.at[which].at[view], target.at[view], out_sems.at[number])
        )
        stores[-1].start()
    for store in stores:
        store.wait()


def widen(summed, factor):
    shape = jax.ShapeDtypeStruct((HALF, TAPS * CH), jnp.float32)
    return pl.pallas_call(
        functools.partial(widen_kernel, factor),
        out_shape=(shape, shape),
        in_specs=[pl.BlockSpec(memory_space=pl.ANY)],
        out_specs=(pl.BlockSpec(memory_space=pl.ANY), pl.BlockSpec(memory_space=pl.ANY)),
        scratch_shapes=[
            pltpu.VMEM((4, HALF, TAPS * HALF), jnp.bfloat16),
            pltpu.VMEM((2, HALF, TAPS * CH), jnp.float32),
            pltpu.SemaphoreType.DMA((6,)),
            pltpu.SemaphoreType.DMA((6,)),
        ],
        compiler_params=pltpu.CompilerParams(vmem_limit_bytes=58 * 2**20),
        name="widen",
    )(summed)


def local(features, cotangent, w_first, w_second):
    factor = 1.0 / math.sqrt(NX * NY * NZ * CELLS_CHIP)
    flow, summed = whole_layer(
        features.transpose(1, 2, 0), cotangent.transpose(1, 2, 0), w_first, w_second
    )
    grad_first, grad_second = widen(summed, factor)
    return (flow.transpose(2, 0, 1), grad_first, grad_second)


def solution(mesh):
    in_specs = (P(None, "az", "grp"), P(None, "az", "grp"), P("grp", None), P("grp", None))
    out_specs = (P(None, "az", "grp"), P("grp", None), P("grp", None))
    return jax.shard_map(local, mesh=mesh, in_specs=in_specs, out_specs=out_specs, check_vma=False)
```

```python
import functools
import math

import jax
import jax.numpy as jnp
from jax import lax
from jax.experimental import pallas as pl
from jax.experimental.pallas import tpu as pltpu
from jax.sharding import PartitionSpec as P

CH = 256
HALF = 128
TAPS = 27
RAD = 16
AXIAL = 8
AZ_DEV = 4
ROWS = RAD * AXIAL
OWN_ROWS = ROWS // 2
CELLS_CHIP = AZ_DEV * ROWS

NX, NY, NZ = 4, 4, 8
EXTENT = {"x": NX, "y": NY, "z": NZ}
TAP_LANES = 128
PARTS = (
    ((1,), "yzx", 0, 2, 1),
    ((1,), "xzy", 2, 4, 1),
    ((1,), "xzy", 6, 6, -1),
    ((1,), "yzx", 12, 6, 1),
    ((0,), "xzy", 0, 6, 1),
    ((0,), "xzy", 6, 6, -1),
    ((0,), "yzx", 12, 6, -1),
    ((0, 1), "yzx", 18, 3, 1),
    ((0, 1), "yzx", 21, 3, 1),
    ((0, 1), "xzy", 24, 3, 1),
)


BYTES_PER_US = 54000.0
SEND_US, HOP_US, STEP_US = 1.75, 0.3, 0.15
CONVOLVE_US, TERMS_US, SHIFT_US = 0.45, 1.0, 1.5


class Links:
    def __init__(self, send_sems, recv_sems):
        self.send_sems, self.recv_sems, self.used, self.started = send_sems, recv_sems, 0, []
        self.now, self.busy = 0.0, {}
        flat = lax.axis_index("az")
        self.flat, self.core = flat, lax.axis_index("grp")
        self.at = {"x": flat % NX, "y": (flat // NX) % NY, "z": flat // (NX * NY)}

    def index(self, axis, shift):
        return (self.at[axis] + (shift + EXTENT[axis])) % EXTENT[axis]

    def peer(self, axis, shift):
        to = dict(self.at)
        to[axis] = self.index(axis, shift)
        return {"az": (to["z"] * NY + to["y"]) * NX + to["x"], "grp": self.core}

    def beside(self, shift, core):
        count = NX * NY * NZ
        return {"az": (self.flat + (shift + count)) % count, "grp": core}

    def copy(self, source, target, axis, shift):
        lane, hops = (axis, shift > 0), abs(shift)
        begin = max(self.now, self.busy.get(lane, 0.0))
        self.busy[lane] = begin + hops * 2 * math.prod(source.shape) / BYTES_PER_US
        handle = self.send(source, target, self.peer(axis, shift))
        return handle, self.busy[lane] + SEND_US + HOP_US * hops

    def send(self, source, target, device):
        number = self.used
        self.used += 1
        handle = pltpu.make_async_remote_copy(
            src_ref=source,
            dst_ref=target,
            send_sem=self.send_sems.at[number],
            recv_sem=self.recv_sems.at[number],
            device_id=device,
            device_id_type=pl.DeviceIdType.MESH,
        )
        handle.start()
        self.started.append(handle)
        return handle


def piece(ref, part, axes, at):
    which, order, tap, taps, _ = part
    split = [axis for axis in order[:2] if axis != "z"][0]
    rows = pl.ds(pl.multiple_of(at["z"] * 16, 16), 16) if "z" in axes else slice(None)
    lanes = pl.ds(tap * TAP_LANES, taps * TAP_LANES)
    if split not in axes:
        return ref.at[pl.ds(2 * which[0], 2 * len(which)), rows, lanes]
    if len(which) == 2:
        return ref.at[at[split], rows, lanes]
    half = taps // 2
    begin = (tap + at[split] % 2 * half) * TAP_LANES
    lanes = pl.ds(pl.multiple_of(begin, TAP_LANES), half * TAP_LANES)
    return ref.at[2 * which[0] + at[split] // 2, rows, lanes]


ROUTES = {4: ((2, 1), (-1, -1)), 8: ((4, 1), (2, 1), (-3, -1), (-1, -1))}


def relays(axis):
    return [(owner - stop, stop) for owner, stop in ROUTES[EXTENT[axis]] if owner != stop]


def arrivals(axis):
    routes = ROUTES[EXTENT[axis]]
    return [onward for onward, _ in relays(axis)] + [o for o, stop in routes if o == stop]


def scatter_axis(links, axis, sense, own, stage, landing):
    first = []
    for slot, (owner, stop) in enumerate(ROUTES[EXTENT[axis]]):
        stage[slot] = own(links.index(axis, sense * owner)).astype(jnp.bfloat16)
        first.append(links.copy(stage.at[slot], landing.at[slot], axis, sense * stop))
    last = []
    slot = len(first)
    for number, (owner, stop) in enumerate(ROUTES[EXTENT[axis]]):
        handle, due = first[number]
        if owner == stop:
            last.append((number, handle, due))
            continue
        onward = owner - stop
        total = own(links.index(axis, sense * onward))
        yield due
        handle.wait_recv()
        stage[slot] = (total + landing[number].astype(jnp.float32)).astype(jnp.bfloat16)
        last.append((slot,) + links.copy(stage.at[slot], landing.at[slot], axis, sense * onward))
        slot += 1
    total = own(links.at[axis])
    yield max(due for _, _, due in last)
    for slot, handle, _ in last:
        handle.wait_recv()
        total = total + landing[slot].astype(jnp.float32)
    return total


def gather_axis(links, axis, sense, view):
    chunk = view(links.at[axis])
    first = [
        (onward,) + links.copy(chunk, chunk, axis, sense * onward) for onward in arrivals(axis)
    ]
    last = []
    for number, (onward, stop) in enumerate(relays(axis)):
        _, handle, due = first[number]
        yield due
        handle.wait_recv()
        chunk = view(links.index(axis, -sense * onward))
        last.append(links.copy(chunk, chunk, axis, sense * stop))
    last += [(handle, due) for _, handle, due in first[len(last) :]]
    yield max(due for _, due in last)
    for handle, _ in last:
        handle.wait_recv()


def reduce_part(links, part, source, result, buffers):
    which, (first, second, third), tap, taps, sense = part
    stage_one, landing_one, sum_one, stage_two, landing_two, landing_three = buffers
    at = links.at

    def own_first(index):
        return piece(source, part, (first,), {first: index})[...]

    sum_one[...] = yield from scatter_axis(
        links, first, sense, own_first, stage_one, landing_one
    )

    def own_second(index):
        if second == "z":
            return sum_one[pl.ds(pl.multiple_of(index * 16, 16), 16), :]
        return sum_one[index]

    total = yield from scatter_axis(links, second, -sense, own_second, stage_two, landing_two)
    mine = landing_three.at[at[third]]
    mine[...] = total.astype(jnp.bfloat16)
    sent = [links.copy(mine, mine, third, shift) for shift in (1, -1, 2)]
    yield max(due for _, due in sent)
    for handle, _ in sent:
        handle.wait_recv()
    total = landing_three[0].astype(jnp.float32)
    for index in range(1, EXTENT[third]):
        total = total + landing_three[index].astype(jnp.float32)
    both = (first, second)
    piece(result, part, both, at)[...] = total.astype(jnp.bfloat16)
    yield from gather_axis(
        links, second, sense, lambda index: piece(result, part, both, {**at, second: index})
    )
    yield from gather_axis(
        links, first, -sense, lambda index: piece(result, part, (first,), {first: index})
    )


def part_scratch(part):
    which, (first, second, third), tap, taps, sense = part
    lanes = taps * TAP_LANES * len(which) // 2
    two = (16, lanes)
    one = (4,) + two if first == "z" else (128, lanes)
    slots = {axis: EXTENT[axis] - 1 for axis in EXTENT}
    return [
        pltpu.VMEM((slots[first],) + one, jnp.bfloat16),
        pltpu.VMEM((slots[first],) + one, jnp.bfloat16),
        pltpu.VMEM(one, jnp.float32),
        pltpu.VMEM((slots[second],) + two, jnp.bfloat16),
        pltpu.VMEM((slots[second],) + two, jnp.bfloat16),
        pltpu.VMEM((EXTENT[third],) + two, jnp.bfloat16),
    ]


def greet(links):
    barrier = pltpu.get_barrier_semaphore()
    peers = [links.peer("z", shift) for shift in (1, -1, 2, -2, 3, -3)]
    peers += [links.beside(0, 1 - links.core)]
    peers += [links.peer(axis, shift) for axis in "xy" for shift in (1, -1, 2)]
    peers += [
        links.beside(shift, core) for shift in (1, -1) for core in (links.core, 1 - links.core)
    ]
    for device in peers:
        pl.semaphore_signal(
            barrier, inc=1, device_id=device, device_id_type=pl.DeviceIdType.MESH
        )
    pl.semaphore_wait(barrier, len(peers))


def shifted_copies(level, padded):
    channels = level.shape[3]
    along = lax.broadcasted_iota(jnp.int32, (RAD, AXIAL, channels), 1)
    rim = jnp.zeros((AXIAL, channels), jnp.bfloat16).astype(jnp.float32)

    def one_slab(slab, carry):
        here = level[1, slab].astype(jnp.float32).reshape(RAD, AXIAL, channels)
        below = jnp.where(along == 0, 0.0, pltpu.roll(here, 1, 1))
        above = jnp.where(along == AXIAL - 1, 0.0, pltpu.roll(here, AXIAL - 1, 1))
        for offset, values in ((0, below), (1, here), (2, above)):
            rows = values.reshape(ROWS, channels)
            if offset != 1:
                level[offset, slab] = rows.astype(jnp.bfloat16)
            padded[offset, slab] = jnp.concatenate((rim, rows, rim), axis=0).astype(jnp.bfloat16)
        return carry

    lax.fori_loop(0, AZ_DEV + 2, one_slab, 0)


def window(level, padded, along_az, along_rad, along_ax):
    channels = level.shape[3]
    slabs = pl.ds(along_az, AZ_DEV)
    if along_rad == 1:
        picked = level[along_ax, slabs]
    else:
        picked = padded[along_ax, slabs, pl.ds(AXIAL * along_rad, ROWS), :]
    return picked.reshape(CELLS_CHIP, channels)


def tap_lanes(along_az, along_rad, along_ax, width):
    tap = (along_az * 3 + along_rad) * 3 + along_ax
    start = tap * width
    return pl.ds(start if isinstance(tap, int) else pl.multiple_of(start, width), width)


def convolve_step(level, padded, weight, total, along_az, along_ax):
    added = total[...]
    for along_rad in range(3):
        added = added + lax.dot_general(
            window(level, padded, along_az, along_rad, along_ax),
            weight[:, tap_lanes(along_az, along_rad, along_ax, CH)],
            (((1,), (1,)), ((), ())),
            preferred_element_type=jnp.float32,
        )
    total[...] = added


def convolve(level, padded, weight, total):
    total[...] = jnp.zeros_like(total)

    def one_step(step, carry):
        convolve_step(level, padded, weight, total, step // 3, step % 3)
        return carry

    lax.fori_loop(0, 9, one_step, 0)


def convolve_back(level, padded, weight, total):
    total[...] = jnp.zeros_like(total)

    def one_step(step, carry):
        along_az, along_ax = step // 3, step % 3
        columns = jnp.concatenate(
            [window(level, padded, 2 - along_az, 2 - rad, 2 - along_ax) for rad in range(3)], axis=1
        )
        rows = jnp.concatenate(
            [weight[:, tap_lanes(along_az, rad, along_ax, CH)] for rad in range(3)], axis=0
        )
        update = jnp.dot(columns, rows, preferred_element_type=jnp.float32)
        for side in range(2):
            total[side] = total[side] + update[:, side * HALF : (side + 1) * HALF]
        return carry

    lax.fori_loop(0, 9, one_step, 0)


def weight_terms(turned, level, padded, terms, which, along_az):
    def one_step(along_ax, carry):
        for along_rad in range(3):
            update = jnp.dot(
                turned[...],
                window(level, padded, along_az, along_rad, along_ax),
                preferred_element_type=jnp.float32,
            )
            lanes = tap_lanes(along_az, along_rad, along_ax, HALF)
            for side in range(2):
                terms[2 * which + side, :, lanes] = update[:, side * HALF : (side + 1) * HALF]
        return carry

    lax.fori_loop(0, 3, one_step, 0)


def flow_part(links, features, level, padded, weight, total, mine, flow):
    core = links.core
    lanes = pl.ds(pl.multiple_of(core * HALF, HALF), HALF)
    total[...] = jnp.zeros_like(total)
    for step in range(9):
        yield None
        convolve_step(level, padded, weight, total, step // 3, step % 3)
        links.now += CONVOLVE_US
    own = features[1, pl.ds(1, AZ_DEV), :, lanes].astype(jnp.float32)
    mine[...] = (own + total[...].reshape(AZ_DEV, ROWS, HALF)).astype(jnp.bfloat16)
    here = pl.ds(pl.multiple_of(core * OWN_ROWS, OWN_ROWS), OWN_ROWS)
    there = pl.ds(pl.multiple_of((1 - core) * OWN_ROWS, OWN_ROWS), OWN_ROWS)
    flow[:, :, lanes] = mine[:, here, :]
    handle = links.send(mine.at[:, there, :], flow.at[:, :, lanes], links.beside(0, 1 - core))
    yield links.now + 60.0
    handle.wait_recv()


def exchange_rims(links, source, target, rows):
    core = links.core
    handles = []
    for to in (1 - core, core):
        for shift, slab, landing in ((1, AZ_DEV - 1, 0), (-1, 0, AZ_DEV + 1)):
            given, taken = source(slab, to), target(landing, to)
            handles.append(links.send(given, taken, links.beside(shift, to)))
        if to is not core:
            handles.append(
                links.send(
                    source(slice(None), to), target(pl.ds(1, AZ_DEV), to), links.beside(0, to)
                )
            )
    return handles


def whole_kernel(
    features,
    cotangent,
    w_first,
    w_second,
    flow,
    result,
    send_sems,
    recv_sems,
    local_sems,
    first_rows,
    second_rows,
    in_level,
    in_padded,
    cot_level,
    cot_padded,
    hid_level,
    hid_padded,
    pre,
    second,
    back,
    back_other,
    turned,
    mine,
    terms,
    held,
    *buffers,
):
    links = Links(send_sems, recv_sems)
    core = links.core
    here = pl.ds(pl.multiple_of(core * OWN_ROWS, OWN_ROWS), OWN_ROWS)
    cells = pl.ds(1, AZ_DEV)

    def lanes(which):
        return pl.ds(pl.multiple_of(which * HALF, HALF), HALF)

    loads = [
        pltpu.make_async_copy(*pair, local_sems.at[number])
        for number, pair in enumerate(
            (
                (features, in_level.at[1, cells, here, :]),
                (cotangent.at[:, :, lanes(core)], cot_level.at[1, cells, here, :]),
                (w_first, first_rows),
                (w_second, second_rows),
            )
        )
    ]
    for load in loads:
        load.start()
    greet(links)
    field_in = exchange_rims(
        links,
        lambda slab, to: features.at[slab],
        lambda slab, to: in_level.at[1, slab, here, :],
        here,
    )
    field_cot = exchange_rims(
        links,
        lambda slab, to: cotangent.at[slab, :, lanes(to)],
        lambda slab, to: cot_level.at[1, slab, here, :],
        here,
    )
    loads[0].wait()
    loads[2].wait()
    for handle in field_in:
        handle.wait_recv()
    shifted_copies(in_level, in_padded)
    convolve(in_level, in_padded, first_rows, pre)
    values = pre[...]
    hidden = values * jax.nn.sigmoid(values)
    hid_level[1, cells, :, lanes(core)] = hidden.astype(jnp.bfloat16).reshape(AZ_DEV, ROWS, HALF)
    field_hid = exchange_rims(
        links,
        lambda slab, to: hid_level.at[
            1, pl.ds(1, AZ_DEV) if isinstance(slab, slice) else slab + 1, :, lanes(core)
        ],
        lambda slab, to: hid_level.at[1, slab, :, lanes(core)],
        here,
    )
    loads[1].wait()
    loads[3].wait()
    for handle in field_cot:
        handle.wait_recv()
    shifted_copies(cot_level, cot_padded)
    convolve_back(cot_level, cot_padded, second_rows, back)
    swap = links.send(back.at[1 - core], back_other, links.beside(0, 1 - core))
    own_cot = cot_level[1, cells].reshape(CELLS_CHIP, HALF).astype(jnp.float32)
    turned[1] = own_cot.T.astype(jnp.bfloat16)
    for handle in field_hid:
        handle.wait_recv()
    shifted_copies(hid_level, hid_padded)
    parts, used = [], 0
    for part in PARTS:
        count = len(part_scratch(part))
        parts.append((part, buffers[used : used + count]))
        used += count
    stored = []

    def one_part(part, scratch):
        yield from reduce_part(links, part, terms, held, scratch)
        done = [piece(ref, part, (), {}) for ref in (held, result)]
        stored.append(pltpu.make_async_copy(*done, local_sems.at[4 + len(stored)]))
        stored[-1].start()

    def gradients():
        ready = set()
        for which in (1, 0):
            if which == 0:
                swap.wait_recv()
                values = pre[...]
                sigma = jax.nn.sigmoid(values)
                slope = (back[core] + back_other[...]) * (sigma * (1.0 + values * (1.0 - sigma)))
                turned[0] = slope.T.astype(jnp.bfloat16)
            level, padded = (in_level, in_padded) if which == 0 else (hid_level, hid_padded)
            for along_az in range(3):
                weight_terms(turned.at[which], level, padded, terms, which, along_az)
                links.now += TERMS_US
                ready |= {(which, 9 * along_az + tap) for tap in range(9)}
                for one in list(parts):
                    grads, _, tap, taps, _ = one[0]
                    if {(g, t) for g in grads for t in range(tap, tap + taps)} <= ready:
                        parts.remove(one)
                        advance(one_part(*one))
                yield 0.0
        advance(flow_part(links, in_level, hid_level, hid_padded, second_rows, second, mine, flow))

    waiting = []

    def advance(one):
        links.now += STEP_US
        try:
            waiting.append((next(one), one))
        except StopIteration:
            pass

    advance(gradients())
    while waiting:
        due = [links.now + CONVOLVE_US if at is None else at or links.now for at, _ in waiting]
        soonest = min(range(len(due)), key=due.__getitem__)
        at, one = waiting.pop(soonest)
        links.now = max(links.now, at or 0.0)
        advance(one)
    for copy in stored:
        copy.wait()
    for handle in links.started:
        handle.wait_send()


COPIES = 256


def whole_layer(features, cotangent, w_first, w_second):
    field = (3, AZ_DEV + 2, ROWS)
    padded = (3, AZ_DEV + 2, ROWS + 2 * AXIAL)
    scratch = [
        pltpu.SemaphoreType.DMA((COPIES,)),
        pltpu.SemaphoreType.DMA((COPIES,)),
        pltpu.SemaphoreType.DMA((4 + len(PARTS),)),
        pltpu.VMEM((HALF, TAPS * CH), jnp.bfloat16),
        pltpu.VMEM((HALF, TAPS * CH), jnp.bfloat16),
        pltpu.VMEM(field + (CH,), jnp.bfloat16),
        pltpu.VMEM(padded + (CH,), jnp.bfloat16),
        pltpu.VMEM(field + (HALF,), jnp.bfloat16),
        pltpu.VMEM(padded + (HALF,), jnp.bfloat16),
        pltpu.VMEM(field + (CH,), jnp.bfloat16),
        pltpu.VMEM(padded + (CH,), jnp.bfloat16),
        pltpu.VMEM((CELLS_CHIP, HALF), jnp.float32),
        pltpu.VMEM((CELLS_CHIP, HALF), jnp.float32),
        pltpu.VMEM((2, CELLS_CHIP, HALF), jnp.float32),
        pltpu.VMEM((CELLS_CHIP, HALF), jnp.float32),
        pltpu.VMEM((2, HALF, CELLS_CHIP), jnp.bfloat16),
        pltpu.VMEM((AZ_DEV, ROWS, HALF), jnp.bfloat16),
        pltpu.VMEM((4, HALF, TAPS * HALF), jnp.float32),
        pltpu.VMEM((4, HALF, TAPS * HALF), jnp.bfloat16),
    ]
    for part in PARTS:
        scratch += part_scratch(part)
    return pl.pallas_call(
        whole_kernel,
        out_shape=(
            jax.ShapeDtypeStruct((AZ_DEV, OWN_ROWS, CH), jnp.bfloat16),
            jax.ShapeDtypeStruct((4, HALF, TAPS * HALF), jnp.bfloat16),
        ),
        in_specs=[pl.BlockSpec(memory_space=pltpu.HBM)] * 4,
        out_specs=(pl.BlockSpec(memory_space=pltpu.VMEM), pl.BlockSpec(memory_space=pl.ANY)),
        scratch_shapes=scratch,
        compiler_params=pltpu.CompilerParams(
            collective_id=0, has_side_effects=True, vmem_limit_bytes=56 * 2**20
        ),
        name="both_layers",
    )(features, cotangent, w_first, w_second)


def widen_kernel(
    factor,
    summed,
    flow,
    grad_first,
    grad_second,
    flow_out,
    taken,
    wide,
    held,
    in_sems,
    out_sems,
):
    pieces = [(which, third) for which in range(2) for third in range(3)]
    loads, stores = [], []
    for number, (which, third) in enumerate(pieces):
        view = (pl.ds(2 * which, 2), slice(None), pl.ds(third * 9 * HALF, 9 * HALF))
        loads.append(
            pltpu.make_async_copy(summed.at[view], taken.at[view], in_sems.at[number])
        )
        loads[-1].start()
    flow_in = pltpu.make_async_copy(flow, held, in_sems.at[len(pieces)])
    flow_in.start()
    for number, (which, third) in enumerate(pieces):
        loads[number].wait()
        for tap in range(9 * third, 9 * third + 9):
            for side in range(2):
                wide[which, :, (2 * tap + side) * HALF : (2 * tap + side + 1) * HALF] = (
                    taken[2 * which + side, :, tap * HALF : (tap + 1) * HALF].astype(jnp.float32)
                    * factor
                )
        view = (slice(None), pl.ds(third * 9 * CH, 9 * CH))
        target = grad_second if which else grad_first
        stores.append(
            pltpu.make_async_copy(wide.at[which].at[view], target.at[view], out_sems.at[number])
        )
        stores[-1].start()
    flow_in.wait()
    stores.append(pltpu.make_async_copy(held, flow_out, out_sems.at[len(pieces)]))
    stores[-1].start()
    for store in stores:
        store.wait()


def widen(summed, flow, factor):
    shape = jax.ShapeDtypeStruct((HALF, TAPS * CH), jnp.float32)
    return pl.pallas_call(
        functools.partial(widen_kernel, factor),
        out_shape=(shape, shape, jax.ShapeDtypeStruct(flow.shape, flow.dtype)),
        in_specs=[pl.BlockSpec(memory_space=pl.ANY)] * 2,
        out_specs=(pl.BlockSpec(memory_space=pl.ANY),) * 3,
        scratch_shapes=[
            pltpu.VMEM((4, HALF, TAPS * HALF), jnp.bfloat16),
            pltpu.VMEM((2, HALF, TAPS * CH), jnp.float32),
            pltpu.VMEM(flow.shape, flow.dtype),
            pltpu.SemaphoreType.DMA((7,)),
            pltpu.SemaphoreType.DMA((7,)),
        ],
        compiler_params=pltpu.CompilerParams(vmem_limit_bytes=58 * 2**20),
        name="widen",
    )(summed, flow)


def local(features, cotangent, w_first, w_second):
    factor = 1.0 / math.sqrt(NX * NY * NZ * CELLS_CHIP)
    flow, summed = whole_layer(
        features.transpose(1, 2, 0), cotangent.transpose(1, 2, 0), w_first, w_second
    )
    grad_first, grad_second, flow = widen(summed, flow, factor)
    return (flow.transpose(2, 0, 1), grad_first, grad_second)


def solution(mesh):
    in_specs = (P(None, "az", "grp"), P(None, "az", "grp"), P("grp", None), P("grp", None))
    out_specs = (P(None, "az", "grp"), P("grp", None), P("grp", None))
    return jax.shard_map(local, mesh=mesh, in_specs=in_specs, out_specs=out_specs, check_vma=False)
```

```python
import functools
import math

import jax
import jax.numpy as jnp
from jax import lax
from jax.experimental import pallas as pl
from jax.experimental.pallas import tpu as pltpu
from jax.sharding import PartitionSpec as P

CH = 256
HALF = 128
TAPS = 27
RAD = 16
AXIAL = 8
AZ_DEV = 4
ROWS = RAD * AXIAL
OWN_ROWS = ROWS // 2
CELLS_CHIP = AZ_DEV * ROWS

NX, NY, NZ = 4, 4, 8
EXTENT = {"x": NX, "y": NY, "z": NZ}
TAP_LANES = 128
PARTS = (
    ((1,), "yzx", 0, 2, 1),
    ((1,), "xzy", 2, 4, 1),
    ((1,), "xzy", 6, 6, -1),
    ((1,), "yzx", 12, 6, 1),
    ((0,), "xzy", 0, 6, 1),
    ((0,), "xzy", 6, 6, -1),
    ((0,), "yzx", 12, 6, -1),
    ((0, 1), "yzx", 18, 3, 1),
    ((0, 1), "yzx", 21, 3, 1),
    ((0, 1), "xzy", 24, 3, 1),
)


BYTES_PER_US = 54000.0
SEND_US, HOP_US, STEP_US = 1.75, 0.3, 0.15
CONVOLVE_US, TERMS_US, SHIFT_US = 0.45, 1.0, 1.5


class Links:
    def __init__(self, send_sems, recv_sems):
        self.send_sems, self.recv_sems, self.used, self.started = send_sems, recv_sems, 0, []
        self.now, self.busy = 0.0, {}
        flat = lax.axis_index("az")
        self.flat, self.core = flat, lax.axis_index("grp")
        self.at = {"x": flat % NX, "y": (flat // NX) % NY, "z": flat // (NX * NY)}

    def index(self, axis, shift):
        return (self.at[axis] + (shift + EXTENT[axis])) % EXTENT[axis]

    def peer(self, axis, shift):
        to = dict(self.at)
        to[axis] = self.index(axis, shift)
        return {"az": (to["z"] * NY + to["y"]) * NX + to["x"], "grp": self.core}

    def beside(self, shift, core):
        count = NX * NY * NZ
        return {"az": (self.flat + (shift + count)) % count, "grp": core}

    def copy(self, source, target, axis, shift):
        lane, hops = (axis, shift > 0), abs(shift)
        begin = max(self.now, self.busy.get(lane, 0.0))
        self.busy[lane] = begin + hops * 2 * math.prod(source.shape) / BYTES_PER_US
        handle = self.send(source, target, self.peer(axis, shift))
        return handle, self.busy[lane] + SEND_US + HOP_US * hops

    def send(self, source, target, device):
        number = self.used
        self.used += 1
        handle = pltpu.make_async_remote_copy(
            src_ref=source,
            dst_ref=target,
            send_sem=self.send_sems.at[number],
            recv_sem=self.recv_sems.at[number],
            device_id=device,
            device_id_type=pl.DeviceIdType.MESH,
        )
        handle.start()
        self.started.append(handle)
        return handle


def piece(ref, part, axes, at):
    which, order, tap, taps, _ = part
    split = [axis for axis in order[:2] if axis != "z"][0]
    rows = pl.ds(pl.multiple_of(at["z"] * 16, 16), 16) if "z" in axes else slice(None)
    lanes = pl.ds(tap * TAP_LANES, taps * TAP_LANES)
    if split not in axes:
        return ref.at[pl.ds(2 * which[0], 2 * len(which)), rows, lanes]
    if len(which) == 2:
        return ref.at[at[split], rows, lanes]
    half = taps // 2
    begin = (tap + at[split] % 2 * half) * TAP_LANES
    lanes = pl.ds(pl.multiple_of(begin, TAP_LANES), half * TAP_LANES)
    return ref.at[2 * which[0] + at[split] // 2, rows, lanes]


ROUTES = {4: ((2, 1), (-1, -1)), 8: ((4, 1), (2, 1), (-3, -1), (-1, -1))}


STRAIGHT = ((2, 2), (1, 1), (-1, -1))
HASTY = (6,)


def routes_of(axis, hasty):
    return STRAIGHT if hasty else ROUTES[EXTENT[axis]]


def relays(axis, hasty):
    return [(owner - stop, stop) for owner, stop in routes_of(axis, hasty) if owner != stop]


def arrivals(axis, hasty):
    routes = routes_of(axis, hasty)
    return [onward for onward, _ in relays(axis, hasty)] + [o for o, stop in routes if o == stop]


def scatter_axis(links, axis, sense, own, stage, landing, hasty=False):
    first = []
    for slot, (owner, stop) in enumerate(routes_of(axis, hasty)):
        stage[slot] = own(links.index(axis, sense * owner)).astype(jnp.bfloat16)
        first.append(links.copy(stage.at[slot], landing.at[slot], axis, sense * stop))
    last = []
    slot = len(first)
    for number, (owner, stop) in enumerate(routes_of(axis, hasty)):
        handle, due = first[number]
        if owner == stop:
            last.append((number, handle, due))
            continue
        onward = owner - stop
        total = own(links.index(axis, sense * onward))
        yield due
        handle.wait_recv()
        stage[slot] = (total + landing[number].astype(jnp.float32)).astype(jnp.bfloat16)
        last.append((slot,) + links.copy(stage.at[slot], landing.at[slot], axis, sense * onward))
        slot += 1
    total = own(links.at[axis])
    yield max(due for _, _, due in last)
    for slot, handle, _ in last:
        handle.wait_recv()
        total = total + landing[slot].astype(jnp.float32)
    return total


def gather_axis(links, axis, sense, view, hasty=False):
    chunk = view(links.at[axis])
    first = [
        (onward,) + links.copy(chunk, chunk, axis, sense * onward) for onward in arrivals(axis, hasty)
    ]
    last = []
    for number, (onward, stop) in enumerate(relays(axis, hasty)):
        _, handle, due = first[number]
        yield due
        handle.wait_recv()
        chunk = view(links.index(axis, -sense * onward))
        last.append(links.copy(chunk, chunk, axis, sense * stop))
    last += [(handle, due) for _, handle, due in first[len(last) :]]
    yield max(due for _, due in last)
    for handle, _ in last:
        handle.wait_recv()


def reduce_part(links, part, source, result, buffers):
    which, (first, second, third), tap, taps, sense = part
    stage_one, landing_one, sum_one, stage_two, landing_two, landing_three = buffers
    at = links.at
    hasty = PARTS.index(part) in HASTY

    def own_first(index):
        return piece(source, part, (first,), {first: index})[...]

    sum_one[...] = yield from scatter_axis(
        links, first, sense, own_first, stage_one, landing_one, hasty
    )

    def own_second(index):
        if second == "z":
            return sum_one[pl.ds(pl.multiple_of(index * 16, 16), 16), :]
        return sum_one[index]

    total = yield from scatter_axis(links, second, -sense, own_second, stage_two, landing_two)
    mine = landing_three.at[at[third]]
    mine[...] = total.astype(jnp.bfloat16)
    sent = [links.copy(mine, mine, third, shift) for shift in (1, -1, 2)]
    yield max(due for _, due in sent)
    for handle, _ in sent:
        handle.wait_recv()
    total = landing_three[0].astype(jnp.float32)
    for index in range(1, EXTENT[third]):
        total = total + landing_three[index].astype(jnp.float32)
    both = (first, second)
    piece(result, part, both, at)[...] = total.astype(jnp.bfloat16)
    yield from gather_axis(
        links, second, sense, lambda index: piece(result, part, both, {**at, second: index})
    )
    yield from gather_axis(
        links, first, -sense, lambda index: piece(result, part, (first,), {first: index}), hasty
    )


def part_scratch(part):
    which, (first, second, third), tap, taps, sense = part
    lanes = taps * TAP_LANES * len(which) // 2
    two = (16, lanes)
    one = (4,) + two if first == "z" else (128, lanes)
    slots = {axis: EXTENT[axis] - 1 for axis in EXTENT}
    return [
        pltpu.VMEM((slots[first],) + one, jnp.bfloat16),
        pltpu.VMEM((slots[first],) + one, jnp.bfloat16),
        pltpu.VMEM(one, jnp.float32),
        pltpu.VMEM((slots[second],) + two, jnp.bfloat16),
        pltpu.VMEM((slots[second],) + two, jnp.bfloat16),
        pltpu.VMEM((EXTENT[third],) + two, jnp.bfloat16),
    ]


def greet(links):
    barrier = pltpu.get_barrier_semaphore()
    peers = [links.peer("z", shift) for shift in (1, -1, 2, -2, 3, -3)]
    peers += [links.beside(0, 1 - links.core)]
    peers += [links.peer(axis, shift) for axis in "xy" for shift in (1, -1, 2)]
    peers += [
        links.beside(shift, core) for shift in (1, -1) for core in (links.core, 1 - links.core)
    ]
    for device in peers:
        pl.semaphore_signal(
            barrier, inc=1, device_id=device, device_id_type=pl.DeviceIdType.MESH
        )
    pl.semaphore_wait(barrier, len(peers))


def shifted_copies(level, padded):
    channels = level.shape[3]
    along = lax.broadcasted_iota(jnp.int32, (RAD, AXIAL, channels), 1)
    rim = jnp.zeros((AXIAL, channels), jnp.bfloat16).astype(jnp.float32)

    def one_slab(slab, carry):
        here = level[1, slab].astype(jnp.float32).reshape(RAD, AXIAL, channels)
        below = jnp.where(along == 0, 0.0, pltpu.roll(here, 1, 1))
        above = jnp.where(along == AXIAL - 1, 0.0, pltpu.roll(here, AXIAL - 1, 1))
        for offset, values in ((0, below), (1, here), (2, above)):
            rows = values.reshape(ROWS, channels)
            if offset != 1:
                level[offset, slab] = rows.astype(jnp.bfloat16)
            padded[offset, slab] = jnp.concatenate((rim, rows, rim), axis=0).astype(jnp.bfloat16)
        return carry

    lax.fori_loop(0, AZ_DEV + 2, one_slab, 0)


def window(level, padded, along_az, along_rad, along_ax):
    channels = level.shape[3]
    slabs = pl.ds(along_az, AZ_DEV)
    if along_rad == 1:
        picked = level[along_ax, slabs]
    else:
        picked = padded[along_ax, slabs, pl.ds(AXIAL * along_rad, ROWS), :]
    return picked.reshape(CELLS_CHIP, channels)


def tap_lanes(along_az, along_rad, along_ax, width):
    tap = (along_az * 3 + along_rad) * 3 + along_ax
    start = tap * width
    return pl.ds(start if isinstance(tap, int) else pl.multiple_of(start, width), width)


def convolve_step(level, padded, weight, total, along_az, along_ax):
    added = total[...]
    for along_rad in range(3):
        added = added + lax.dot_general(
            window(level, padded, along_az, along_rad, along_ax),
            weight[:, tap_lanes(along_az, along_rad, along_ax, CH)],
            (((1,), (1,)), ((), ())),
            preferred_element_type=jnp.float32,
        )
    total[...] = added


def convolve(level, padded, weight, total):
    total[...] = jnp.zeros_like(total)

    def one_step(step, carry):
        convolve_step(level, padded, weight, total, step // 3, step % 3)
        return carry

    lax.fori_loop(0, 9, one_step, 0)


def convolve_back(level, padded, weight, total):
    total[...] = jnp.zeros_like(total)

    def one_step(step, carry):
        along_az, along_ax = step // 3, step % 3
        columns = jnp.concatenate(
            [window(level, padded, 2 - along_az, 2 - rad, 2 - along_ax) for rad in range(3)], axis=1
        )
        rows = jnp.concatenate(
            [weight[:, tap_lanes(along_az, rad, along_ax, CH)] for rad in range(3)], axis=0
        )
        update = jnp.dot(columns, rows, preferred_element_type=jnp.float32)
        for side in range(2):
            total[side] = total[side] + update[:, side * HALF : (side + 1) * HALF]
        return carry

    lax.fori_loop(0, 9, one_step, 0)


def weight_terms(turned, level, padded, terms, which, along_az):
    def one_step(along_ax, carry):
        for along_rad in range(3):
            update = jnp.dot(
                turned[...],
                window(level, padded, along_az, along_rad, along_ax),
                preferred_element_type=jnp.float32,
            )
            lanes = tap_lanes(along_az, along_rad, along_ax, HALF)
            for side in range(2):
                terms[2 * which + side, :, lanes] = update[:, side * HALF : (side + 1) * HALF]
        return carry

    lax.fori_loop(0, 3, one_step, 0)


def flow_part(links, features, level, padded, weight, total, mine, flow):
    core = links.core
    lanes = pl.ds(pl.multiple_of(core * HALF, HALF), HALF)
    total[...] = jnp.zeros_like(total)
    for step in range(9):
        yield None
        convolve_step(level, padded, weight, total, step // 3, step % 3)
        links.now += CONVOLVE_US
    own = features[1, pl.ds(1, AZ_DEV), :, lanes].astype(jnp.float32)
    mine[...] = (own + total[...].reshape(AZ_DEV, ROWS, HALF)).astype(jnp.bfloat16)
    here = pl.ds(pl.multiple_of(core * OWN_ROWS, OWN_ROWS), OWN_ROWS)
    there = pl.ds(pl.multiple_of((1 - core) * OWN_ROWS, OWN_ROWS), OWN_ROWS)
    flow[:, :, lanes] = mine[:, here, :]
    handle = links.send(mine.at[:, there, :], flow.at[:, :, lanes], links.beside(0, 1 - core))
    yield links.now + 60.0
    handle.wait_recv()


def exchange_rims(links, source, target, rows):
    core = links.core
    handles = []
    for to in (1 - core, core):
        for shift, slab, landing in ((1, AZ_DEV - 1, 0), (-1, 0, AZ_DEV + 1)):
            given, taken = source(slab, to), target(landing, to)
            handles.append(links.send(given, taken, links.beside(shift, to)))
        if to is not core:
            handles.append(
                links.send(
                    source(slice(None), to), target(pl.ds(1, AZ_DEV), to), links.beside(0, to)
                )
            )
    return handles


def whole_kernel(
    features,
    cotangent,
    w_first,
    w_second,
    flow,
    result,
    send_sems,
    recv_sems,
    local_sems,
    first_rows,
    second_rows,
    in_level,
    in_padded,
    cot_level,
    cot_padded,
    hid_level,
    hid_padded,
    pre,
    second,
    back,
    back_other,
    turned,
    mine,
    terms,
    held,
    *buffers,
):
    links = Links(send_sems, recv_sems)
    core = links.core
    here = pl.ds(pl.multiple_of(core * OWN_ROWS, OWN_ROWS), OWN_ROWS)
    cells = pl.ds(1, AZ_DEV)

    def lanes(which):
        return pl.ds(pl.multiple_of(which * HALF, HALF), HALF)

    loads = [
        pltpu.make_async_copy(*pair, local_sems.at[number])
        for number, pair in enumerate(
            (
                (features, in_level.at[1, cells, here, :]),
                (cotangent.at[:, :, lanes(core)], cot_level.at[1, cells, here, :]),
                (w_first, first_rows),
                (w_second, second_rows),
            )
        )
    ]
    for load in loads:
        load.start()
    greet(links)
    field_in = exchange_rims(
        links,
        lambda slab, to: features.at[slab],
        lambda slab, to: in_level.at[1, slab, here, :],
        here,
    )
    field_cot = exchange_rims(
        links,
        lambda slab, to: cotangent.at[slab, :, lanes(to)],
        lambda slab, to: cot_level.at[1, slab, here, :],
        here,
    )
    loads[0].wait()
    loads[2].wait()
    for handle in field_in:
        handle.wait_recv()
    shifted_copies(in_level, in_padded)
    convolve(in_level, in_padded, first_rows, pre)
    values = pre[...]
    hidden = values * jax.nn.sigmoid(values)
    hid_level[1, cells, :, lanes(core)] = hidden.astype(jnp.bfloat16).reshape(AZ_DEV, ROWS, HALF)
    field_hid = exchange_rims(
        links,
        lambda slab, to: hid_level.at[
            1, pl.ds(1, AZ_DEV) if isinstance(slab, slice) else slab + 1, :, lanes(core)
        ],
        lambda slab, to: hid_level.at[1, slab, :, lanes(core)],
        here,
    )
    loads[1].wait()
    loads[3].wait()
    for handle in field_cot:
        handle.wait_recv()
    shifted_copies(cot_level, cot_padded)
    convolve_back(cot_level, cot_padded, second_rows, back)
    swap = links.send(back.at[1 - core], back_other, links.beside(0, 1 - core))
    own_cot = cot_level[1, cells].reshape(CELLS_CHIP, HALF).astype(jnp.float32)
    turned[1] = own_cot.T.astype(jnp.bfloat16)
    for handle in field_hid:
        handle.wait_recv()
    shifted_copies(hid_level, hid_padded)
    parts, used = [], 0
    for part in PARTS:
        count = len(part_scratch(part))
        parts.append((part, buffers[used : used + count]))
        used += count
    stored = []

    def one_part(part, scratch):
        yield from reduce_part(links, part, terms, held, scratch)
        done = [piece(ref, part, (), {}) for ref in (held, result)]
        stored.append(pltpu.make_async_copy(*done, local_sems.at[4 + len(stored)]))
        stored[-1].start()

    def gradients():
        ready = set()
        for which in (1, 0):
            if which == 0:
                swap.wait_recv()
                values = pre[...]
                sigma = jax.nn.sigmoid(values)
                slope = (back[core] + back_other[...]) * (sigma * (1.0 + values * (1.0 - sigma)))
                turned[0] = slope.T.astype(jnp.bfloat16)
            level, padded = (in_level, in_padded) if which == 0 else (hid_level, hid_padded)
            for along_az in range(3):
                weight_terms(turned.at[which], level, padded, terms, which, along_az)
                links.now += TERMS_US
                ready |= {(which, 9 * along_az + tap) for tap in range(9)}
                for one in list(parts):
                    grads, _, tap, taps, _ = one[0]
                    if {(g, t) for g in grads for t in range(tap, tap + taps)} <= ready:
                        parts.remove(one)
                        advance(one_part(*one))
                yield 0.0
        advance(flow_part(links, in_level, hid_level, hid_padded, second_rows, second, mine, flow))

    waiting = []

    def advance(one):
        links.now += STEP_US
        try:
            waiting.append((next(one), one))
        except StopIteration:
            pass

    advance(gradients())
    while waiting:
        due = [links.now + CONVOLVE_US if at is None else at or links.now for at, _ in waiting]
        soonest = min(range(len(due)), key=due.__getitem__)
        at, one = waiting.pop(soonest)
        links.now = max(links.now, at or 0.0)
        advance(one)
    for copy in stored:
        copy.wait()
    for handle in links.started:
        handle.wait_send()


COPIES = 256


def whole_layer(features, cotangent, w_first, w_second):
    field = (3, AZ_DEV + 2, ROWS)
    padded = (3, AZ_DEV + 2, ROWS + 2 * AXIAL)
    scratch = [
        pltpu.SemaphoreType.DMA((COPIES,)),
        pltpu.SemaphoreType.DMA((COPIES,)),
        pltpu.SemaphoreType.DMA((4 + len(PARTS),)),
        pltpu.VMEM((HALF, TAPS * CH), jnp.bfloat16),
        pltpu.VMEM((HALF, TAPS * CH), jnp.bfloat16),
        pltpu.VMEM(field + (CH,), jnp.bfloat16),
        pltpu.VMEM(padded + (CH,), jnp.bfloat16),
        pltpu.VMEM(field + (HALF,), jnp.bfloat16),
        pltpu.VMEM(padded + (HALF,), jnp.bfloat16),
        pltpu.VMEM(field + (CH,), jnp.bfloat16),
        pltpu.VMEM(padded + (CH,), jnp.bfloat16),
        pltpu.VMEM((CELLS_CHIP, HALF), jnp.float32),
        pltpu.VMEM((CELLS_CHIP, HALF), jnp.float32),
        pltpu.VMEM((2, CELLS_CHIP, HALF), jnp.float32),
        pltpu.VMEM((CELLS_CHIP, HALF), jnp.float32),
        pltpu.VMEM((2, HALF, CELLS_CHIP), jnp.bfloat16),
        pltpu.VMEM((AZ_DEV, ROWS, HALF), jnp.bfloat16),
        pltpu.VMEM((4, HALF, TAPS * HALF), jnp.float32),
        pltpu.VMEM((4, HALF, TAPS * HALF), jnp.bfloat16),
    ]
    for part in PARTS:
        scratch += part_scratch(part)
    return pl.pallas_call(
        whole_kernel,
        out_shape=(
            jax.ShapeDtypeStruct((AZ_DEV, OWN_ROWS, CH), jnp.bfloat16),
            jax.ShapeDtypeStruct((4, HALF, TAPS * HALF), jnp.bfloat16),
        ),
        in_specs=[pl.BlockSpec(memory_space=pltpu.HBM)] * 4,
        out_specs=(pl.BlockSpec(memory_space=pltpu.VMEM), pl.BlockSpec(memory_space=pl.ANY)),
        scratch_shapes=scratch,
        compiler_params=pltpu.CompilerParams(
            collective_id=0, has_side_effects=True, vmem_limit_bytes=56 * 2**20
        ),
        name="both_layers",
    )(features, cotangent, w_first, w_second)


def widen_kernel(
    factor,
    summed,
    flow,
    grad_first,
    grad_second,
    flow_out,
    taken,
    wide,
    held,
    in_sems,
    out_sems,
):
    pieces = [(which, third) for which in range(2) for third in range(3)]
    loads, stores = [], []
    for number, (which, third) in enumerate(pieces):
        view = (pl.ds(2 * which, 2), slice(None), pl.ds(third * 9 * HALF, 9 * HALF))
        loads.append(
            pltpu.make_async_copy(summed.at[view], taken.at[view], in_sems.at[number])
        )
        loads[-1].start()
    flow_in = pltpu.make_async_copy(flow, held, in_sems.at[len(pieces)])
    flow_in.start()
    for number, (which, third) in enumerate(pieces):
        loads[number].wait()
        for tap in range(9 * third, 9 * third + 9):
            for side in range(2):
                wide[which, :, (2 * tap + side) * HALF : (2 * tap + side + 1) * HALF] = (
                    taken[2 * which + side, :, tap * HALF : (tap + 1) * HALF].astype(jnp.float32)
                    * factor
                )
        view = (slice(None), pl.ds(third * 9 * CH, 9 * CH))
        target = grad_second if which else grad_first
        stores.append(
            pltpu.make_async_copy(wide.at[which].at[view], target.at[view], out_sems.at[number])
        )
        stores[-1].start()
    flow_in.wait()
    stores.append(pltpu.make_async_copy(held, flow_out, out_sems.at[len(pieces)]))
    stores[-1].start()
    for store in stores:
        store.wait()


def widen(summed, flow, factor):
    shape = jax.ShapeDtypeStruct((HALF, TAPS * CH), jnp.float32)
    return pl.pallas_call(
        functools.partial(widen_kernel, factor),
        out_shape=(shape, shape, jax.ShapeDtypeStruct(flow.shape, flow.dtype)),
        in_specs=[pl.BlockSpec(memory_space=pl.ANY)] * 2,
        out_specs=(pl.BlockSpec(memory_space=pl.ANY),) * 3,
        scratch_shapes=[
            pltpu.VMEM((4, HALF, TAPS * HALF), jnp.bfloat16),
            pltpu.VMEM((2, HALF, TAPS * CH), jnp.float32),
            pltpu.VMEM(flow.shape, flow.dtype),
            pltpu.SemaphoreType.DMA((7,)),
            pltpu.SemaphoreType.DMA((7,)),
        ],
        compiler_params=pltpu.CompilerParams(vmem_limit_bytes=58 * 2**20),
        name="widen",
    )(summed, flow)


def local(features, cotangent, w_first, w_second):
    factor = 1.0 / math.sqrt(NX * NY * NZ * CELLS_CHIP)
    flow, summed = whole_layer(
        features.transpose(1, 2, 0), cotangent.transpose(1, 2, 0), w_first, w_second
    )
    grad_first, grad_second, flow = widen(summed, flow, factor)
    return (flow.transpose(2, 0, 1), grad_first, grad_second)


def solution(mesh):
    in_specs = (P(None, "az", "grp"), P(None, "az", "grp"), P("grp", None), P("grp", None))
    out_specs = (P(None, "az", "grp"), P("grp", None), P("grp", None))
    return jax.shard_map(local, mesh=mesh, in_specs=in_specs, out_specs=out_specs, check_vma=False)
```
